256 devices in a mesh: ctx: 64 (over z, x, core), head: 4 (over y).
Axes of the slice: x: 4, y: 4, z: 8, core: 2. Of those that a mesh axis runs over, the one named last changes fastest.
Arguments:
- query_rows: bfloat16 [32768, 4096], P('ctx', 'head'), may hold values from -1.75 to 1.75
- key_rows: bfloat16 [32768, 4096], P('ctx', 'head'), may hold values from -1.75 to 1.75
- value_rows: bfloat16 [32768, 4096], P('ctx', 'head'), may hold values from -6 to 6
- gate_rows: bfloat16 [32768, 4096], P('ctx', 'head'), may hold values from -8 to 8
- init_state: float32 [32, 128, 128], P('head'), may hold values from -192 to 192
- decay_rate: float32 [32], P('head'), as said below
- norm_gain: float32 [4096], P('head'), may hold values from 0.1 to 1.9
- out_weight: bfloat16 [4096, 6144], P('head', 'ctx'), may hold values from -0.25 to 0.25
Outputs:
- mixed: bfloat16 [32768, 6144], P('ctx', 'head')
The draws below stay inside these ranges and needn't reach their ends.
Inputs may be any that keep to these rules, and one draw needn't show every extreme that they name: `decay_rate`: each rate is positive, between 0.05 / 32768 and 1/30.
All inputs are finite; a program needn't handle non-finite values.
Results may differ from the reference program's by a relative error of at most 0.015.
Values may be sent and summed in bfloat16 or wider, within the bound.
A program may use at most 128 MiB of HBM per device.

```python
import jax
import jax.numpy as jnp
from jax import lax

HEADS = 32
HD = 128
DM = 6144
BLOCK = 256
LENGTH = 32768
TOKENS = 32768
N_HEAD = 4


def draw_decay_rate(key, part):
    key = jax.random.fold_in(key, 7)
    key_order, key_jitter = jax.random.split(key)
    slow_share = 0.5
    slow_count = max(1, int(slow_share * HEADS))
    fast_count = max(1, HEADS - slow_count)
    rank = jax.random.permutation(key_order, HEADS).astype(jnp.float32)
    jitter = jax.random.uniform(key_jitter, (HEADS,), jnp.float32)
    slow_low = jnp.log(jnp.float32(0.05) / LENGTH)
    slow_high = jnp.log(jnp.float32(2.0) / LENGTH)
    fast_low = jnp.log(jnp.float32(1.0 / 2000.0))
    fast_high = jnp.log(jnp.float32(1.0 / 30.0))
    slow_place = (rank + jitter) / slow_count
    fast_place = jnp.clip((rank - slow_count + jitter) / fast_count, 0.0, 1.0)
    slow_log = slow_low + (slow_high - slow_low) * slow_place
    fast_log = fast_low + (fast_high - fast_low) * fast_place
    return jnp.exp(jnp.where(rank < slow_count, slow_log, fast_log)).astype(jnp.float32)


def with_spikes(entries, stream_key, source, target, parts, factor):
    def block_of(dim):
        return (jnp.arange(entries.shape[dim]) // (entries.shape[dim] // parts)).reshape((-1,) + (1,) * (entries.ndim - 1 - dim))

    one_side = jax.random.permutation(stream_key, parts)[block_of(target)]
    other_side = (block_of(target) + parts // 2) % parts
    return jnp.where((block_of(source) == one_side) | (block_of(source) == other_side), factor * entries, entries)


def steps_of(stream_key, shape, shards, smallest, high):
    def one(dim, parts):
        steps = jax.random.uniform(jax.random.fold_in(jax.random.fold_in(stream_key, 6), dim), (parts,), jnp.float32, smallest / len(shards), high / len(shards))
        return jnp.repeat(jnp.exp(steps), shape[dim] // parts).reshape((-1,) + (1,) * (len(shape) - dim - 1))

    gain = one(*shards[0])
    for cut in shards[1:]:
        gain = gain * one(*cut)
    return gain


def bell_draw(stream_key, dims, spread, most, cuts=(), held_as=jnp.bfloat16):
    drawn = jax.random.normal(stream_key, dims, jnp.float32) * spread
    if len(cuts) > 0:
        drawn = steps_of(stream_key, dims, cuts, -0.22, 0.18) * drawn
    return jnp.clip(drawn, min=-most, max=most).astype(held_as)


def heavy_noise(stream_key, shape, spread, limit, cuts, heavy, held_as=jnp.bfloat16):
    result = spread * jax.random.normal(stream_key, shape, jnp.float32)
    if cuts:
        result = result * steps_of(stream_key, shape, cuts, -0.22, 0.18)
    return jnp.clip(with_spikes(result, jax.random.fold_in(stream_key, 3), *heavy), -limit, limit).astype(held_as)


def setup_inputs(seed: int = 0) -> dict:
    streams_of = jax.random.split(jax.random.key(seed), 9)
    return {
        "query_rows": bell_draw(streams_of[0], (TOKENS, HEADS * HD), 0.3, 1.75, ((0, 64), (1, 4))),
        "key_rows": bell_draw(streams_of[1], (TOKENS, HEADS * HD), 0.3, 1.75, ((0, 64), (1, 4))),
        "value_rows": bell_draw(streams_of[2], (TOKENS, HEADS * HD), 1.0, 6.0, ((0, 64), (1, 4))),
        "gate_rows": bell_draw(streams_of[3], (TOKENS, HEADS * HD), 1.5, 8.0, ((0, 64), (1, 4))),
        "init_state": bell_draw(streams_of[4], (HEADS, HD, HD), 32.0, 192.0, ((0, 4),), jnp.float32),
        "decay_rate": draw_decay_rate(jax.random.fold_in(streams_of[8], 71), 0),
        "norm_gain": jnp.clip(1.0 + 0.18 * jax.random.normal(streams_of[6], (HEADS * HD,), jnp.float32), 0.1, 1.9),
        "out_weight": heavy_noise(streams_of[7], (HEADS * HD, DM), (HEADS * HD) ** -0.5, 0.25, ((0, 4), (1, 64)), (0, 1, 64, 4.0)),
    }


def reference(query_rows, key_rows, value_rows, gate_rows, init_state, decay_rate, norm_gain, out_weight):
    block_len = BLOCK
    block_count = TOKENS // block_len
    shape_four = (block_count, block_len, HEADS, HD)
    query_blocks = query_rows.reshape(shape_four)
    key_blocks = key_rows.reshape(shape_four)
    value_blocks = value_rows.reshape(shape_four)
    gate_blocks = gate_rows.reshape(block_count, block_len, HEADS * HD)
    position = jnp.arange(block_len, dtype=jnp.float32)
    offset = position[:, None] - position[None, :]
    decay_mat = jnp.where(offset[None] >= 0.0, jnp.exp(-decay_rate[:, None, None] * jnp.maximum(offset, 0.0)[None]), 0.0)
    into_weight = jnp.exp(-decay_rate[None, :] * (position[:, None] + 1.0))
    key_weight = jnp.exp(-decay_rate[None, :] * (block_len - 1.0 - position)[:, None])
    block_decay = jnp.exp(-decay_rate * block_len)
    group_width = HEADS * HD // N_HEAD
    highest = lax.Precision.HIGHEST

    def advance(state, inputs):
        q_blk, k_blk, v_blk, g_blk = inputs
        scores = jnp.einsum('ihd,jhd->hij', q_blk.astype(jnp.float32), k_blk.astype(jnp.float32))
        weights_bf = (scores * decay_mat).astype(jnp.bfloat16)
        intra = jnp.einsum('hij,jhd->ihd', weights_bf.astype(jnp.float32), v_blk.astype(jnp.float32))
        inter = jnp.einsum('ihd,hde->ihe', q_blk.astype(jnp.float32), state, precision=highest) * into_weight[:, :, None]
        keyed = k_blk.astype(jnp.float32) * key_weight[:, :, None]
        contrib = jnp.einsum('jhd,jhe->hde', keyed, v_blk.astype(jnp.float32), precision=highest)
        new_state = block_decay[:, None, None] * state + contrib
        attn = intra + inter
        scale = lax.rsqrt(lax.optimization_barrier(jnp.mean(attn * attn, axis=-1, keepdims=True)) + 1e-06)
        normed = (attn * scale).reshape(block_len, HEADS * HD)
        hidden = (normed * norm_gain[None, :] * jax.nn.sigmoid(g_blk.astype(jnp.float32))).astype(jnp.bfloat16)
        total = jnp.zeros((block_len, DM), jnp.float32)
        for group in range(N_HEAD):
            part = jnp.dot(hidden[:, group * group_width:(group + 1) * group_width], out_weight[group * group_width:(group + 1) * group_width], preferred_element_type=jnp.float32)
            part_bf = lax.optimization_barrier(part.astype(jnp.bfloat16))
            total = total + part_bf.astype(jnp.float32)
        return (new_state, total.astype(jnp.bfloat16))
    final_state, outputs = lax.scan(advance, init_state, (query_blocks, key_blocks, value_blocks, gate_blocks))
    return outputs.reshape(TOKENS, DM)
```

```python
import jax
import jax.numpy as jnp
from jax import lax
from jax.sharding import PartitionSpec as P
from jax.experimental import pallas as pl
from jax.experimental.pallas import tpu as pltpu

MESH = pl.DeviceIdType.MESH
F32 = jnp.float32
BF16 = jnp.bfloat16
HD = 128
BLK = 256
ROWS = 512
NH = 8


def dot(a, b, ca=1, cb=0):
    return lax.dot_general(a, b, (((ca,), (cb,)), ((), ())), preferred_element_type=F32)


def kernel(
    rate, gain, init, q_hbm, k_hbm, v_hbm, g_hbm, hid,
    q, k, v, g, u, gs, c0, loc, rx1, exc, tx2, rx2, tx3, rx3,
    lsem, s1, r1, s2, r2, s3, r3,
):
    c = lax.axis_index("ctx")
    y = lax.axis_index("head")
    z = c // 8
    me = c % 8

    barrier = pltpu.get_barrier_semaphore()
    for d in range(1, 8):
        pl.semaphore_signal(
            barrier, inc=1, device_id=(z * 8 + (me + d) % 8, y), device_id_type=MESH
        )
        pl.semaphore_signal(
            barrier, inc=1, device_id=(((z + d) % 8) * 8 + me, y), device_id_type=MESH
        )
    loads = [
        pltpu.make_async_copy(a, b, lsem.at[i])
        for i, (a, b) in enumerate(((k_hbm, k), (v_hbm, v), (q_hbm, q), (g_hbm, g)))
    ]
    for cp in loads:
        cp.start()
    loads[0].wait()
    loads[1].wait()

    col = lax.broadcasted_iota(jnp.int32, (BLK, HD), 0).astype(F32)

    for h in range(NH):
        r = rate[h]
        hs = slice(h * HD, (h + 1) * HD)
        kw = jnp.exp(-r * (BLK - 1.0 - col))
        k0 = (k[0:BLK, hs].astype(F32) * kw).astype(BF16)
        k1 = (k[BLK:ROWS, hs].astype(F32) * kw).astype(BF16)
        a0 = dot(k0, v[0:BLK, hs], 0, 0)
        a1 = dot(k1, v[BLK:ROWS, hs], 0, 0)
        c0[h] = a0.astype(BF16)
        loc[h] = (jnp.exp(jnp.full((1, HD), -r * BLK)) * a0 + a1).astype(BF16)

    rx1[me] = loc[me]
    pl.semaphore_wait(barrier, 14)
    sends = []
    for d in range(1, 8):
        to = (me + d) % 8
        cp = pltpu.make_async_remote_copy(
            src_ref=loc.at[to], dst_ref=rx1.at[me], send_sem=s1.at[d - 1],
            recv_sem=r1.at[me], device_id=(z * 8 + to, y), device_id_type=MESH,
        )
        cp.start()
        sends.append(cp)

    loads[2].wait()
    loads[3].wait()
    ii = lax.broadcasted_iota(jnp.int32, (BLK, BLK), 0)
    jj = lax.broadcasted_iota(jnp.int32, (BLK, BLK), 1)
    off = (ii - jj).astype(F32)

    def intra(h):
        r = rate[h]
        hs = slice(h * HD, (h + 1) * HD)
        decay = jnp.where(off >= 0.0, jnp.exp(-r * jnp.maximum(off, 0.0)), 0.0)
        for b in range(2):
            rs = slice(b * BLK, (b + 1) * BLK)
            w = (dot(q[rs, hs], k[rs, hs], 1, 1) * decay).astype(BF16)
            o = dot(w, v[rs, hs])
            if b == 1:
                o = o + jnp.exp(-r * (col + 1.0)) * dot(q[rs, hs], c0[h])
            u[rs, hs] = o
        gs[:, hs] = jax.nn.sigmoid(g[:, hs].astype(F32)) * gain[:, hs]

    for h in range(3):
        intra(h)

    for d in range(1, 8):
        p = (me + 8 - d) % 8
        pltpu.make_async_remote_copy(
            src_ref=loc.at[0], dst_ref=rx1.at[p], send_sem=s1.at[0],
            recv_sem=r1.at[p], device_id=(z * 8 + p, y), device_id_type=MESH,
        ).wait_recv()
    rm = rate[me]
    d512 = jnp.exp(jnp.full((1, HD), -rm * 512.0))
    e = jnp.zeros((HD, HD), F32)
    for p in range(8):
        exc[p] = e
        e = d512 * e + rx1[p].astype(F32)
    tx2[...] = e.astype(BF16)
    for d in range(1, 8):
        @pl.when(z + d < 8)
        def _():
            pltpu.make_async_remote_copy(
                src_ref=tx2, dst_ref=rx2.at[z], send_sem=s2.at[d - 1],
                recv_sem=r2.at[z], device_id=((z + d) % 8 * 8 + me, y), device_id_type=MESH,
            ).start()

    for h in range(3, NH):
        intra(h)

    tx3[...] = init[me]
    for i in range(7):
        @pl.when(i < z)
        def _():
            pltpu.make_async_remote_copy(
                src_ref=tx2, dst_ref=rx2.at[i], send_sem=s2.at[0],
                recv_sem=r2.at[i], device_id=(i * 8 + me, y), device_id_type=MESH,
            ).wait_recv()
            tx3[...] = jnp.exp(jnp.full((1, HD), -rm * 4096.0)) * tx3[...] + rx2[i].astype(F32)
    base = tx3[...]
    for p in range(8):
        rx1[p] = (jnp.exp(jnp.full((1, HD), -rm * (512.0 * p))) * base + exc[p]).astype(BF16)
    rx3[me] = rx1[me]
    for d in range(1, 8):
        to = (me + d) % 8
        cp = pltpu.make_async_remote_copy(
            src_ref=rx1.at[to], dst_ref=rx3.at[me], send_sem=s3.at[d - 1],
            recv_sem=r3.at[me], device_id=(z * 8 + to, y), device_id_type=MESH,
        )
        cp.start()
        sends.append(cp)

    row = lax.broadcasted_iota(jnp.int32, (ROWS, HD), 0).astype(F32)
    for h in range(NH):
        @pl.when(h != me)
        def _():
            pltpu.make_async_remote_copy(
                src_ref=rx1.at[0], dst_ref=rx3.at[h], send_sem=s3.at[0],
                recv_sem=r3.at[h], device_id=(z * 8 + h, y), device_id_type=MESH,
            ).wait_recv()
        hs = slice(h * HD, (h + 1) * HD)
        at = u[:, hs] + jnp.exp(-rate[h] * (row + 1.0)) * dot(q[:, hs], rx3[h])
        scale = lax.rsqrt(jnp.mean(at * at, axis=-1, keepdims=True) + 1e-06)
        hid[:, hs] = (at * scale * gs[:, hs]).astype(BF16)

    for cp in sends:
        cp.wait_send()
    for d in range(1, 8):
        @pl.when(z + d < 8)
        def _():
            pltpu.make_async_remote_copy(
                src_ref=tx2, dst_ref=rx2.at[z], send_sem=s2.at[d - 1],
                recv_sem=r2.at[z], device_id=((z + d) % 8 * 8 + me, y), device_id_type=MESH,
            ).wait_send()


def body(
    query_rows, key_rows, value_rows, gate_rows, init_state, decay_rate, norm_gain, out_weight
):
    vm = pl.BlockSpec(memory_space=pltpu.VMEM)
    anyspace = pl.BlockSpec(memory_space=pl.ANY)
    dma = pltpu.SemaphoreType.DMA
    hidden = pl.pallas_call(
        kernel,
        out_shape=jax.ShapeDtypeStruct((ROWS, NH * HD), BF16),
        in_specs=[pl.BlockSpec(memory_space=pltpu.SMEM), vm, vm] + [anyspace] * 4,
        out_specs=vm,
        scratch_shapes=[
            pltpu.VMEM((ROWS, NH * HD), BF16),
            pltpu.VMEM((ROWS, NH * HD), BF16),
            pltpu.VMEM((ROWS, NH * HD), BF16),
            pltpu.VMEM((ROWS, NH * HD), BF16),
            pltpu.VMEM((ROWS, NH * HD), F32),
            pltpu.VMEM((ROWS, NH * HD), F32),
            pltpu.VMEM((NH, HD, HD), BF16),
            pltpu.VMEM((NH, HD, HD), BF16),
            pltpu.VMEM((8, HD, HD), BF16),
            pltpu.VMEM((8, HD, HD), F32),
            pltpu.VMEM((HD, HD), BF16),
            pltpu.VMEM((8, HD, HD), BF16),
            pltpu.VMEM((HD, HD), F32),
            pltpu.VMEM((NH, HD, HD), BF16),
            dma((4,)), dma((7,)), dma((8,)), dma((7,)), dma((8,)), dma((7,)), dma((8,)),
        ],
        compiler_params=pltpu.CompilerParams(
            collective_id=0, has_side_effects=True, vmem_limit_bytes=40 * 2**20
        ),
        cost_estimate=pl.CostEstimate(flops=10**9, bytes_accessed=6 * 2**20, transcendentals=10**6),
    )(decay_rate, norm_gain[None, :], init_state, query_rows, key_rows, value_rows, gate_rows)
    terms = jnp.dot(
        hidden,
        lax.all_gather(out_weight, "ctx", axis=1, tiled=True),
        preferred_element_type=F32,
    )
    return lax.psum_scatter(terms.astype(BF16), "head", scatter_dimension=1, tiled=True)


def solution(mesh):
    return jax.shard_map(
        body,
        mesh=mesh,
        in_specs=(
            P("ctx", "head"),
            P("ctx", "head"),
            P("ctx", "head"),
            P("ctx", "head"),
            P("head", None, None),
            P("head"),
            P("head"),
            P("head", "ctx"),
        ),
        out_specs=P("ctx", "head"),
        check_vma=False,
    )
```

```python
import jax
import jax.numpy as jnp
from jax import lax
from jax.sharding import PartitionSpec as P
from jax.experimental import pallas as pl
from jax.experimental.pallas import tpu as pltpu

MESH = pl.DeviceIdType.MESH
F32 = jnp.float32
BF16 = jnp.bfloat16
HD = 128
BLK = 256
ROWS = 512
NH = 8


def dot(a, b, ca=1, cb=0):
    return lax.dot_general(a, b, (((ca,), (cb,)), ((), ())), preferred_element_type=F32)

ORD = (0, 1, 3, 2)


def kernel(
    rate, gain, init, q_hbm, k_hbm, v_hbm, g_hbm, w_hbm, out,
    q, k, v, g, u, gs, c0, loc, rx1, exc, tx2, rx2, tx3, rx3, zb, wt, hidg, acc,
    lsem, s1, r1, s2, r2, s3, r3,
    su, ru, sd, rd, sy, ry, sxu, rxu, sxd, rxd, srl, rrl, szp, rzp, s2d, r2d,
    shu, rhu, shd, rhd, shr, rhr,
):
    c = lax.axis_index("ctx")
    y = lax.axis_index("head")
    z = c // 8
    me = c % 8
    x = me // 2
    core = me % 2
    par = z % 2
    xup, xdn, xop = (x + 1) % 4, (x + 3) % 4, (x + 2) % 4

    def dev(zz, xx, yy, cc=core):
        return (zz * 8 + xx * 2 + cc, yy)

    def rcopy(src, dst, ss, rs, to):
        return pltpu.make_async_remote_copy(
            src_ref=src, dst_ref=dst, send_sem=ss, recv_sem=rs, device_id=to, device_id_type=MESH
        )

    barrier = pltpu.get_barrier_semaphore()
    for d in range(1, 8):
        pl.semaphore_signal(
            barrier, inc=1, device_id=(z * 8 + (me + d) % 8, y), device_id_type=MESH
        )
        pl.semaphore_signal(
            barrier, inc=1, device_id=(((z + d) % 8) * 8 + me, y), device_id_type=MESH
        )
    for d in range(1, 4):
        pl.semaphore_signal(barrier, inc=1, device_id=(c, (y + d) % 4), device_id_type=MESH)
    loads = [
        pltpu.make_async_copy(a, b, lsem.at[i])
        for i, (a, b) in enumerate(
            (
                (k_hbm, k), (v_hbm, v), (w_hbm, zb.at[z]), (q_hbm, q), (g_hbm, g),
                (init.at[me], tx3),
            )
        )
    ]
    for cp in loads:
        cp.start()

    def z_send(s):
        if s == 0:
            rcopy(zb.at[z], zb.at[z], su.at[0], ru.at[0], dev((z + 1) % 8, x, y)).start()
            rcopy(zb.at[z], zb.at[z], sd.at[0], rd.at[0], dev((z + 7) % 8, x, y)).start()
            return
        lo, hi = (z + 8 - s) % 8, (z + s) % 8
        for part in (0, 1):
            zs = lo if part == 0 else hi
            sems = (su, ru) if part == 0 else (sd, rd)
            to = dev((z + 1) % 8 if part == 0 else (z + 7) % 8, x, y)
            if s == 4:
                rows = pl.ds(48 * part, 48)
                rcopy(zb.at[zs, rows], zb.at[zs, rows], sems[0].at[3], sems[1].at[3], to).wait_recv()
            else:
                rcopy(zb.at[zs], zb.at[zs], sems[0].at[s - 1], sems[1].at[s - 1], to).wait_recv()
                if s == 3:
                    rows = pl.ds(48 * part, 48)
                    rcopy(zb.at[zs, rows], zb.at[zs, rows], sems[0].at[3], sems[1].at[3], to).start()
                else:
                    rcopy(zb.at[zs], zb.at[zs], sems[0].at[s], sems[1].at[s], to).start()

    def y_copy(zs):
        j = zs % 2
        return rcopy(zb.at[zs], wt.at[y, x, j, core], sy.at[zs], ry.at[y, j], dev(z, x, zs // 2))

    def y_send(zs):
        j = zs % 2

        @pl.when(zs // 2 == y)
        def _():
            pltpu.make_async_copy(zb.at[zs], wt.at[y, x, j, core], ry.at[y, j]).start()

        @pl.when(zs // 2 != y)
        def _():
            y_copy(zs).start()

    def z_event(s):
        z_send(s)
        y_send((z + 8 - s) % 8)
        if s in (1, 2, 3):
            y_send((z + s) % 8)

    def dist(j):
        d = (2 * y + j + 8 - z) % 8
        return jnp.minimum(d, 8 - d)

    first = jnp.where(dist(0) < dist(1), 0, 1)

    def piece(i, quarter, j):
        return wt.at[(y + ORD[i]) % 4, quarter, j, core]

    def up_copy(i, j):
        p = piece(i, x, j)
        return rcopy(p, p, sxu.at[j, i], rxu.at[j, i], dev(z, xup, y))

    def dn_copy(i, j):
        p = piece(i, x, j)
        return rcopy(p, p, sxd.at[j, i], rxd.at[j, i], dev(z, xdn, y))

    def pair_copy(which, i, j):
        quarter = (x, xdn, xup, xop)[which]
        p = wt.at[(y + order_at(i)) % 4, quarter, j, core]
        return rcopy(p, p, s2d.at[which, j, i], r2d.at[which, j, i], dev(z, x, y, 1 - core))

    def order_at(i):
        if isinstance(i, int):
            return ORD[i]
        return jnp.where(i == 3, 2, jnp.where(i == 2, 3, i))

    def x_send(j):
        for i in range(4):
            yy = (y + ORD[i]) % 4
            rcopy(
                zb.at[0], wt.at[yy, x, j, core], sy.at[0], ry.at[yy, j], dev(z, x, (y + 1) % 4)
            ).wait_recv()
            up_copy(i, j).start()
            dn_copy(i, j).start()
            pair_copy(0, i, j).start()

    def x_stage(s):
        for j in range(2):
            @pl.when(dist(j) == s)
            def _():
                x_send(j)

    def relay_copy(m, j):
        i = 2 * par + m
        quarter, to = (xdn, xup) if m == 0 else (xup, xdn)
        p = wt.at[(y + order_at(i)) % 4, quarter, j, core]
        return rcopy(p, p, srl.at[j, m], rrl.at[j, m], dev(z, to, y))

    def x_event(n):
        j = first if n < 4 else 1 - first
        i = n % 4
        up_copy(i, j).wait_recv()
        pair_copy(1, i, j).start()
        if i % 2 == 0:
            @pl.when(par == i // 2)
            def _():
                relay_copy(0, j).start()
        dn_copy(i, j).wait_recv()
        pair_copy(2, i, j).start()
        if i % 2 == 1:
            @pl.when(par == i // 2)
            def _():
                relay_copy(1, j).start()

    def zpair_copy(m, j, mine):
        i = 2 * par + m if mine else 2 * (1 - par) + m
        p = wt.at[(y + order_at(i)) % 4, xop, j, core]
        return rcopy(p, p, szp.at[j, m], rzp.at[j, m], dev(z + 1 - 2 * par, x, y))

    def opposite_event(n):
        j = first if n < 2 else 1 - first
        m = n % 2
        p = wt.at[(y + order_at(2 * par + m)) % 4, xop, j, core]
        rcopy(p, p, srl.at[j, m], rrl.at[j, m], dev(z, xup, y)).wait_recv()
        zpair_copy(m, j, True).start()
        pair_copy(3, 2 * par + m, j).start()

    def zpair_event(n):
        j = first if n < 2 else 1 - first
        m = n % 2
        zpair_copy(m, j, False).wait_recv()
        pair_copy(3, 2 * (1 - par) + m, j).start()

    def pair_wait(which):
        for j in range(2):
            for i in range(4):
                pair_copy_in(which, i, j).wait_recv()

    def pair_copy_in(which, i, j):
        quarter = (x, xdn, xup, xop)[which]
        p = wt.at[(y + ORD[i]) % 4, quarter, j, 1 - core]
        return rcopy(p, p, s2d.at[which, j, i], r2d.at[which, j, i], dev(z, x, y, 1 - core))

    yup, ydn, yop = (y + 1) % 4, (y + 3) % 4, (y + 2) % 4

    def chunk(who, n):
        return hidg.at[who, :, pl.ds(n * 256, 256)]

    def h_up(n):
        return rcopy(chunk(y, n), chunk(y, n), shu.at[n], rhu.at[n], dev(z, x, yup))

    def h_dn(n):
        return rcopy(chunk(y, n), chunk(y, n), shd.at[n], rhd.at[n], dev(z, x, ydn))

    def h_relay(n):
        who, to = (ydn, yup) if n < 2 else (yup, ydn)
        return rcopy(chunk(who, n), chunk(who, n), shr.at[n], rhr.at[n], dev(z, x, to))

    def h_event(n):
        h_up(n).wait_recv()
        if n < 2:
            h_relay(n).start()
        h_dn(n).wait_recv()
        if n >= 2:
            h_relay(n).start()

    def unit(who, quarter, start=False):
        t = dot(hidg[who], wt[who, quarter].reshape(384, 1024), 1, 1)
        acc[quarter] = t if start else acc[quarter] + t

    loads[0].wait()
    loads[1].wait()
    col = lax.broadcasted_iota(jnp.int32, (BLK, HD), 0).astype(F32)
    for h in range(NH):
        r = rate[h]
        hs = slice(h * HD, (h + 1) * HD)
        kw = jnp.exp(-r * (BLK - 1.0 - col))
        k0 = (k[0:BLK, hs].astype(F32) * kw).astype(BF16)
        k1 = (k[BLK:ROWS, hs].astype(F32) * kw).astype(BF16)
        a0 = dot(k0, v[0:BLK, hs], 0, 0)
        a1 = dot(k1, v[BLK:ROWS, hs], 0, 0)
        c0[h] = a0.astype(BF16)
        loc[h] = (jnp.exp(jnp.full((1, HD), -r * BLK)) * a0 + a1).astype(BF16)

    rx1[me] = loc[me]
    loads[2].wait()
    pl.semaphore_wait(barrier, 17)
    sends = []
    for d in range(1, 8):
        to = (me + d) % 8
        cp = rcopy(loc.at[to], rx1.at[me], s1.at[d - 1], r1.at[me], (z * 8 + to, y))
        cp.start()
        sends.append(cp)
    z_send(0)
    y_send(z)

    loads[3].wait()
    loads[4].wait()
    loads[5].wait()
    ii = lax.broadcasted_iota(jnp.int32, (BLK, BLK), 0)
    jj = lax.broadcasted_iota(jnp.int32, (BLK, BLK), 1)
    off = (ii - jj).astype(F32)

    def intra(h):
        r = rate[h]
        hs = slice(h * HD, (h + 1) * HD)
        decay = jnp.where(off >= 0.0, jnp.exp(-r * jnp.maximum(off, 0.0)), 0.0)
        for b in range(2):
            rs = slice(b * BLK, (b + 1) * BLK)
            w = (dot(q[rs, hs], k[rs, hs], 1, 1) * decay).astype(BF16)
            o = dot(w, v[rs, hs])
            if b == 1:
                o = o + jnp.exp(-r * (col + 1.0)) * dot(q[rs, hs], c0[h])
            u[rs, hs] = o
        gs[:, hs] = jax.nn.sigmoid(g[:, hs].astype(F32)) * gain[:, hs]

    for h in range(3):
        intra(h)

    for d in range(1, 8):
        p = (me + 8 - d) % 8
        rcopy(loc.at[0], rx1.at[p], s1.at[0], r1.at[p], (z * 8 + p, y)).wait_recv()
    rm = rate[me]
    d512 = jnp.exp(jnp.full((1, HD), -rm * 512.0))
    e = jnp.zeros((HD, HD), F32)
    for p in range(8):
        exc[p] = e
        e = d512 * e + rx1[p].astype(F32)
    tx2[...] = e.astype(BF16)

    def z_state(d):
        return rcopy(tx2, rx2.at[z], s2.at[d - 1], r2.at[z], ((z + d) % 8 * 8 + me, y))

    for d in range(1, 8):
        @pl.when(z + d < 8)
        def _():
            z_state(d).start()

    z_event(1)
    for h in range(3, 6):
        intra(h)
    z_event(2)
    x_stage(0)
    x_stage(1)
    for h in range(6, NH):
        intra(h)

    for i in range(7):
        @pl.when(i < z)
        def _():
            rcopy(tx2, rx2.at[i], s2.at[0], r2.at[i], (i * 8 + me, y)).wait_recv()
            tx3[...] = jnp.exp(jnp.full((1, HD), -rm * 4096.0)) * tx3[...] + rx2[i].astype(F32)
    base = tx3[...]
    for p in range(8):
        rx1[p] = (jnp.exp(jnp.full((1, HD), -rm * (512.0 * p))) * base + exc[p]).astype(BF16)
    rx3[me] = rx1[me]
    for d in range(1, 8):
        to = (me + d) % 8
        cp = rcopy(rx1.at[to], rx3.at[me], s3.at[d - 1], r3.at[me], (z * 8 + to, y))
        cp.start()
        sends.append(cp)

    z_event(3)
    x_stage(2)

    row = lax.broadcasted_iota(jnp.int32, (ROWS, HD), 0).astype(F32)
    for h in range(NH):
        @pl.when(h != me)
        def _():
            rcopy(rx1.at[0], rx3.at[h], s3.at[0], r3.at[h], (z * 8 + h, y)).wait_recv()
        hs = slice(h * HD, (h + 1) * HD)
        at = u[:, hs] + jnp.exp(-rate[h] * (row + 1.0)) * dot(q[:, hs], rx3[h])
        scale = lax.rsqrt(jnp.mean(at * at, axis=-1, keepdims=True) + 1e-06)
        hidg[y, :, hs] = (at * scale * gs[:, hs]).astype(BF16)
        if h % 2 == 1:
            h_up(h // 2).start()
            h_dn(h // 2).start()

    z_event(4)
    x_stage(3)
    x_stage(4)

    x_event(0)
    x_event(1)
    pair_wait(0)
    unit(y, x, True)
    x_event(2)
    h_event(0)
    x_event(3)
    h_event(1)
    x_event(4)
    h_event(2)
    x_event(5)
    h_event(3)
    unit(yup, x)
    unit(ydn, x)
    x_event(6)
    x_event(7)
    pair_wait(1)
    for who in (y, ydn, yup):
        unit(who, xdn, who is y)
    pair_wait(2)
    for who in (y, ydn, yup):
        unit(who, xup, who is y)
    for n in range(4):
        opposite_event(n)
    for n in range(4):
        who, to = (yop, yup) if n < 2 else (yop, ydn)
        rcopy(chunk(yop, n), chunk(yop, n), shr.at[n], rhr.at[n], dev(z, x, to)).wait_recv()
    for quarter in (x, xdn, xup):
        unit(yop, quarter)
    for n in range(4):
        zpair_event(n)
    pair_wait(3)
    for who in (y, ydn, yup, yop):
        unit(who, xop, who is y)

    low = lax.broadcasted_iota(jnp.int32, (64, HD), 1) < 64

    def swap(t):
        return pltpu.roll(t, 64, axis=1)

    for pr in range(2):
        for rb in range(8):
            rs = slice(rb * 64, (rb + 1) * 64)
            p0, p1, p2 = (acc[2 * pr, rs, n * HD : (n + 1) * HD] for n in range(3))
            q0, q1, q2 = (acc[2 * pr + 1, rs, n * HD : (n + 1) * HD] for n in range(3))
            sp1, sp2, sq0, sq1 = swap(p1), swap(p2), swap(q0), swap(q1)
            tiles = (
                (p0, jnp.where(low, p1, sq0), jnp.where(low, sq0, sq1)),
                (jnp.where(low, sp1, sp2), jnp.where(low, sp2, q1), q2),
            )
            for j in range(2):
                for n in range(3):
                    at = j * 768 + pr * 384 + n * HD
                    out[rs, at : at + HD] = tiles[j][n].astype(BF16)

    for cp in sends:
        cp.wait_send()
    for d in range(1, 8):
        @pl.when(z + d < 8)
        def _():
            z_state(d).wait_send()
    for s in range(3):
        rcopy(zb.at[0], zb.at[0], su.at[s], ru.at[s], dev((z + 1) % 8, x, y)).wait_send()
        rcopy(zb.at[0], zb.at[0], sd.at[s], rd.at[s], dev((z + 7) % 8, x, y)).wait_send()
    half = zb.at[0, pl.ds(0, 48)]
    rcopy(half, half, su.at[3], ru.at[3], dev((z + 1) % 8, x, y)).wait_send()
    rcopy(half, half, sd.at[3], rd.at[3], dev((z + 7) % 8, x, y)).wait_send()
    for zs in range(8):
        @pl.when(zs // 2 != y)
        def _():
            y_copy(zs).wait_send()
    for j in range(2):
        for i in range(4):
            up_copy(i, j).wait_send()
            dn_copy(i, j).wait_send()
            for which in range(4):
                pair_copy(which, i, j).wait_send()
        for m in range(2):
            relay_copy(m, j).wait_send()
            zpair_copy(m, j, True).wait_send()
    for n in range(4):
        h_up(n).wait_send()
        h_dn(n).wait_send()
        h_relay(n).wait_send()


def body(
    query_rows, key_rows, value_rows, gate_rows, init_state, decay_rate, norm_gain, out_weight
):
    vm = pl.BlockSpec(memory_space=pltpu.VMEM)
    anyspace = pl.BlockSpec(memory_space=pl.ANY)
    dma = pltpu.SemaphoreType.DMA
    return pl.pallas_call(
        kernel,
        out_shape=jax.ShapeDtypeStruct((ROWS, 1536), BF16),
        in_specs=[pl.BlockSpec(memory_space=pltpu.SMEM), vm] + [anyspace] * 6,
        out_specs=vm,
        scratch_shapes=[
            pltpu.VMEM((ROWS, NH * HD), BF16),
            pltpu.VMEM((ROWS, NH * HD), BF16),
            pltpu.VMEM((ROWS, NH * HD), BF16),
            pltpu.VMEM((ROWS, NH * HD), BF16),
            pltpu.VMEM((ROWS, NH * HD), F32),
            pltpu.VMEM((ROWS, NH * HD), F32),
            pltpu.VMEM((NH, HD, HD), BF16),
            pltpu.VMEM((NH, HD, HD), BF16),
            pltpu.VMEM((8, HD, HD), BF16),
            pltpu.VMEM((8, HD, HD), F32),
            pltpu.VMEM((HD, HD), BF16),
            pltpu.VMEM((8, HD, HD), BF16),
            pltpu.VMEM((HD, HD), F32),
            pltpu.VMEM((NH, HD, HD), BF16),
            pltpu.VMEM((8, 96, 1024), BF16),
            pltpu.VMEM((4, 4, 2, 2, 96, 1024), BF16),
            pltpu.VMEM((4, ROWS, NH * HD), BF16),
            pltpu.VMEM((4, ROWS, 384), F32),
            dma((6,)), dma((7,)), dma((8,)), dma((7,)), dma((8,)), dma((7,)), dma((8,)),
            dma((4,)), dma((4,)), dma((4,)), dma((4,)), dma((8,)), dma((4, 2)),
            dma((2, 4)), dma((2, 4)), dma((2, 4)), dma((2, 4)),
            dma((2, 2)), dma((2, 2)), dma((2, 2)), dma((2, 2)),
            dma((4, 2, 4)), dma((4, 2, 4)),
            dma((4,)), dma((4,)), dma((4,)), dma((4,)), dma((4,)), dma((4,)),
        ],
        compiler_params=pltpu.CompilerParams(
            collective_id=0, has_side_effects=True, vmem_limit_bytes=60 * 2**20
        ),
        cost_estimate=pl.CostEstimate(
            flops=8 * 10**9, bytes_accessed=6 * 2**20, transcendentals=10**6
        ),
    )(
        decay_rate, norm_gain[None, :], init_state, query_rows, key_rows, value_rows, gate_rows,
        out_weight.T,
    )


def solution(mesh):
    return jax.shard_map(
        body,
        mesh=mesh,
        in_specs=(
            P("ctx", "head"),
            P("ctx", "head"),
            P("ctx", "head"),
            P("ctx", "head"),
            P("head", None, None),
            P("head"),
            P("head"),
            P("head", "ctx"),
        ),
        out_specs=P("ctx", "head"),
        check_vma=False,
    )
```

```python
import jax
import jax.numpy as jnp
from jax import lax
from jax.sharding import PartitionSpec as P
from jax.experimental import pallas as pl
from jax.experimental.pallas import tpu as pltpu

MESH = pl.DeviceIdType.MESH
F32 = jnp.float32
BF16 = jnp.bfloat16
HD = 128
BLK = 256
ROWS = 512
NH = 8


def dot(a, b, ca=1, cb=0):
    return lax.dot_general(a, b, (((ca,), (cb,)), ((), ())), preferred_element_type=F32)

ORD = (0, 1, 3, 2)


def kernel(
    rate, gain, init, q_hbm, k_hbm, v_hbm, g_hbm, w_hbm, out,
    q, k, v, g, u, gs, c0, loc, rx1, exc, tx2, rx2, tx3, rx3, zb, wt, hidg, acc,
    lsem, s1, r1, s2, r2, s3, r3,
    sz, rz, sy, ry, sx, rx, srl, rrl, szp, rzp, s2d, r2d,
    shu, rhu, shd, rhd, shr, rhr,
):
    c = lax.axis_index("ctx")
    y = lax.axis_index("head")
    z = c // 8
    me = c % 8
    x = me // 2
    core = me % 2
    par = z % 2
    xup, xdn, xop = (x + 1) % 4, (x + 3) % 4, (x + 2) % 4

    def dev(zz, xx, yy, cc=core):
        return (zz * 8 + xx * 2 + cc, yy)

    def rcopy(src, dst, ss, rs, to):
        return pltpu.make_async_remote_copy(
            src_ref=src, dst_ref=dst, send_sem=ss, recv_sem=rs, device_id=to, device_id_type=MESH
        )

    barrier = pltpu.get_barrier_semaphore()
    for d in range(1, 8):
        pl.semaphore_signal(
            barrier, inc=1, device_id=(z * 8 + (me + d) % 8, y), device_id_type=MESH
        )
        pl.semaphore_signal(
            barrier, inc=1, device_id=(((z + d) % 8) * 8 + me, y), device_id_type=MESH
        )
    for d in range(1, 4):
        pl.semaphore_signal(barrier, inc=1, device_id=(c, (y + d) % 4), device_id_type=MESH)
    loads = [
        pltpu.make_async_copy(a, b, lsem.at[i])
        for i, (a, b) in enumerate(
            (
                (k_hbm, k), (v_hbm, v), (w_hbm, zb.at[z]), (q_hbm, q), (g_hbm, g),
                (init.at[me], tx3),
            )
        )
    ]
    for cp in loads:
        cp.start()

    def half(n):
        return pl.ds(48 * n, 48)

    def z_copy(way, zs, n, s):
        p = zb.at[zs, half(n)]
        to = dev((z + 1) % 8 if way == 0 else (z + 7) % 8, x, y)
        return rcopy(p, p, sz.at[way, s, n], rz.at[way, s, n], to)

    def z_start():
        for n in range(2):
            for way in range(2):
                z_copy(way, z, n, 0).start()
            y_send(z, n)

    def y_copy(zs, n):
        return rcopy(
            zb.at[zs, half(n)], wt.at[y, x, zs % 2, core, half(n)],
            sy.at[zs, n], ry.at[y, zs % 2, n], dev(z, x, zs // 2),
        )

    def y_send(zs, n):
        @pl.when(zs // 2 == y)
        def _():
            pltpu.make_async_copy(
                zb.at[zs, half(n)], wt.at[y, x, zs % 2, core, half(n)], ry.at[y, zs % 2, n]
            ).start()

        @pl.when(zs // 2 != y)
        def _():
            y_copy(zs, n).start()

    def z_event(s, n):
        for way in range(2):
            if s == 4 and way != n:
                continue
            zs = (z + 8 - s) % 8 if way == 0 else (z + s) % 8
            z_copy(way, zs, n, s - 1).wait_recv()
            if s < 3 or (s == 3 and way == n):
                z_copy(way, zs, n, s).start()
            y_send(zs, n)

    def dist(j):
        d = (2 * y + j + 8 - z) % 8
        return jnp.minimum(d, 8 - d)

    first = jnp.where(dist(0) < dist(1), 0, 1)
    second = 1 - first

    def order_at(i):
        if isinstance(i, int):
            return ORD[i]
        return jnp.where(i == 3, 2, jnp.where(i == 2, 3, i))

    def piece(i, quarter, j):
        return wt.at[(y + order_at(i)) % 4, quarter, j, core]

    urgent = (2 * par, 2 * par + 1)
    common = ((1, 3), (0, 2))
    toward, source = (xup, xdn), (xdn, xup)

    def x_copy(way, i, j):
        p = piece(i, x, j)
        return rcopy(p, p, sx.at[way, j, i], rx.at[way, j, i], dev(z, toward[way], y))

    def pair_copy(which, i, j):
        p = piece(i, (x, xdn, xup, xop)[which], j)
        return rcopy(p, p, s2d.at[which, j, i], r2d.at[which, j, i], dev(z, x, y, 1 - core))

    def pair_wait(which):
        for j in range(2):
            for i in range(4):
                pair_copy(which, i, j).wait_recv()

    def relay_copy(way, j):
        p = piece(urgent[way], source[way], j)
        return rcopy(p, p, srl.at[j, way], rrl.at[j, way], dev(z, toward[way], y))

    def zpair_copy(w, j, mine=True):
        i = (2 * par if mine else 2 * (1 - par)) + w % 2
        p = piece(i, (xdn, xup, xop, xop)[w], j)
        return rcopy(p, p, szp.at[j, w], rzp.at[j, w], dev(z + 1 - 2 * par, x, y))

    def x_send(j):
        for i in range(4):
            for n in range(2):
                yy = (y + ORD[i]) % 4
                rcopy(
                    zb.at[0, half(n)], wt.at[yy, x, j, core, half(n)], sy.at[0, n],
                    ry.at[yy, j, n], dev(z, x, (y + 1) % 4),
                ).wait_recv()
        for way in range(2):
            x_copy(way, urgent[way], j).start()
        for way in range(2):
            x_copy(way, common[way][0], j).start()
        for i in range(4):
            pair_copy(0, i, j).start()

    def x_stage(s):
        for j in range(2):
            @pl.when(dist(j) == s)
            def _():
                x_send(j)

    def urgent_event(j):
        for way in range(2):
            x_copy(way, urgent[way], j).wait_recv()
            relay_copy(way, j).start()
            zpair_copy(way, j).start()
            pair_copy(1 + way, urgent[way], j).start()

    def common_start(j):
        for way in range(2):
            x_copy(way, common[way][1], j).start()

    def common_event(n, j):
        for way in range(2):
            x_copy(way, common[way][n], j).wait_recv()
            pair_copy(1 + way, common[way][n], j).start()

    def opposite_event(j):
        for way in range(2):
            relay_copy(way, j).wait_recv()
            zpair_copy(2 + way, j).start()
            pair_copy(3, urgent[way], j).start()

    def zpair_event(w, j):
        zpair_copy(w, j, False).wait_recv()
        pair_copy((1, 2, 3, 3)[w], 2 * (1 - par) + w % 2, j).start()

    yup, ydn, yop = (y + 1) % 4, (y + 3) % 4, (y + 2) % 4

    def chunk(who, n):
        return hidg.at[who, :, pl.ds(n * 256, 256)]

    def h_up(n):
        return rcopy(chunk(y, n), chunk(y, n), shu.at[n], rhu.at[n], dev(z, x, yup))

    def h_dn(n):
        return rcopy(chunk(y, n), chunk(y, n), shd.at[n], rhd.at[n], dev(z, x, ydn))

    def h_relay(n):
        who, to = (ydn, yup) if n < 2 else (yup, ydn)
        return rcopy(chunk(who, n), chunk(who, n), shr.at[n], rhr.at[n], dev(z, x, to))

    def h_relay_in(n):
        return rcopy(
            chunk(yop, n), chunk(yop, n), shr.at[n], rhr.at[n], dev(z, x, yup if n < 2 else ydn)
        )

    def h_event(n):
        h_up(n).wait_recv()
        if n < 2:
            h_relay(n).start()
        h_dn(n).wait_recv()
        if n >= 2:
            h_relay(n).start()

    def unit(who, quarter, start=False):
        t = dot(hidg[who], wt[who, quarter].reshape(384, 1024), 1, 1)
        acc[quarter] = t if start else acc[quarter] + t

    loads[0].wait()
    loads[1].wait()
    col = lax.broadcasted_iota(jnp.int32, (BLK, HD), 0).astype(F32)
    def contribs(h):
        r = rate[h]
        hs = slice(h * HD, (h + 1) * HD)
        kw = jnp.exp(-r * (BLK - 1.0 - col))
        k0 = (k[0:BLK, hs].astype(F32) * kw).astype(BF16)
        k1 = (k[BLK:ROWS, hs].astype(F32) * kw).astype(BF16)
        a0 = dot(k0, v[0:BLK, hs], 0, 0)
        a1 = dot(k1, v[BLK:ROWS, hs], 0, 0)
        c0[h] = a0.astype(BF16)
        loc[h] = (jnp.exp(jnp.full((1, HD), -r * BLK)) * a0 + a1).astype(BF16)

    for h in range(4):
        contribs(h)
    loads[2].wait()
    pl.semaphore_wait(barrier, 17)
    z_start()
    for h in range(4, NH):
        contribs(h)
    rx1[me] = loc[me]
    sends = []
    for d in range(1, 8):
        to = (me + d) % 8
        cp = rcopy(loc.at[to], rx1.at[me], s1.at[d - 1], r1.at[me], (z * 8 + to, y))
        cp.start()
        sends.append(cp)

    loads[3].wait()
    loads[4].wait()
    loads[5].wait()
    ii = lax.broadcasted_iota(jnp.int32, (BLK, BLK), 0)
    jj = lax.broadcasted_iota(jnp.int32, (BLK, BLK), 1)
    off = (ii - jj).astype(F32)

    def intra(h):
        r = rate[h]
        hs = slice(h * HD, (h + 1) * HD)
        decay = jnp.where(off >= 0.0, jnp.exp(-r * jnp.maximum(off, 0.0)), 0.0)
        for b in range(2):
            rs = slice(b * BLK, (b + 1) * BLK)
            w = (dot(q[rs, hs], k[rs, hs], 1, 1) * decay).astype(BF16)
            o = dot(w, v[rs, hs])
            if b == 1:
                o = o + jnp.exp(-r * (col + 1.0)) * dot(q[rs, hs], c0[h])
            u[rs, hs] = o
        gs[:, hs] = jax.nn.sigmoid(g[:, hs].astype(F32)) * gain[:, hs]

    intra(0)
    z_event(1, 0)
    z_event(1, 1)
    for d in range(1, 8):
        p = (me + 8 - d) % 8
        rcopy(loc.at[0], rx1.at[p], s1.at[0], r1.at[p], (z * 8 + p, y)).wait_recv()
    rm = rate[me]
    d512 = jnp.exp(jnp.full((1, HD), -rm * 512.0))
    e = jnp.zeros((HD, HD), F32)
    for p in range(8):
        exc[p] = e
        e = d512 * e + rx1[p].astype(F32)
    tx2[...] = e.astype(BF16)

    def z_state(d):
        return rcopy(tx2, rx2.at[z], s2.at[d - 1], r2.at[z], ((z + d) % 8 * 8 + me, y))

    for d in range(1, 8):
        @pl.when(z + d < 8)
        def _():
            z_state(d).start()

    intra(1)
    z_event(2, 0)
    intra(2)
    z_event(2, 1)
    x_stage(0)
    intra(3)
    intra(4)
    z_event(3, 0)
    intra(5)
    z_event(3, 1)
    x_stage(1)
    intra(6)
    intra(7)

    for i in range(7):
        @pl.when(i < z)
        def _():
            rcopy(tx2, rx2.at[i], s2.at[0], r2.at[i], (i * 8 + me, y)).wait_recv()
            tx3[...] = jnp.exp(jnp.full((1, HD), -rm * 4096.0)) * tx3[...] + rx2[i].astype(F32)
    base = tx3[...]
    for p in range(8):
        rx1[p] = (jnp.exp(jnp.full((1, HD), -rm * (512.0 * p))) * base + exc[p]).astype(BF16)
    rx3[me] = rx1[me]
    for d in range(1, 8):
        to = (me + d) % 8
        cp = rcopy(rx1.at[to], rx3.at[me], s3.at[d - 1], r3.at[me], (z * 8 + to, y))
        cp.start()
        sends.append(cp)

    z_event(4, 0)
    z_event(4, 1)
    x_stage(2)
    x_stage(3)

    row = lax.broadcasted_iota(jnp.int32, (ROWS, HD), 0).astype(F32)
    for h in range(NH):
        @pl.when(h != me)
        def _():
            rcopy(rx1.at[0], rx3.at[h], s3.at[0], r3.at[h], (z * 8 + h, y)).wait_recv()
        hs = slice(h * HD, (h + 1) * HD)
        at = u[:, hs] + jnp.exp(-rate[h] * (row + 1.0)) * dot(q[:, hs], rx3[h])
        scale = lax.rsqrt(jnp.mean(at * at, axis=-1, keepdims=True) + 1e-06)
        hidg[y, :, hs] = (at * scale * gs[:, hs]).astype(BF16)
        if h % 2 == 1:
            h_up(h // 2).start()
            h_dn(h // 2).start()

    x_stage(4)

    urgent_event(first)
    pair_wait(0)
    unit(y, x, True)
    urgent_event(second)
    common_start(first)
    h_event(0)
    common_event(0, first)
    opposite_event(first)
    common_start(second)
    h_event(1)
    common_event(0, second)
    opposite_event(second)
    h_event(2)
    for j in (first, second):
        for w in range(2):
            zpair_event(w, j)
    h_event(3)
    unit(yup, x)
    unit(ydn, x)
    common_event(1, first)
    common_event(1, second)
    pair_wait(1)
    for who in (y, ydn, yup):
        unit(who, xdn, who is y)
    pair_wait(2)
    for who in (y, ydn, yup):
        unit(who, xup, who is y)
    for w in range(2, 4):
        zpair_event(w, first)
    for n in range(4):
        h_relay_in(n).wait_recv()
    for quarter in (x, xdn, xup):
        unit(yop, quarter)
    for w in range(2, 4):
        zpair_event(w, second)
    pair_wait(3)
    for who in (y, ydn, yup, yop):
        unit(who, xop, who is y)

    low = lax.broadcasted_iota(jnp.int32, (64, HD), 1) < 64

    def swap(t):
        return pltpu.roll(t, 64, axis=1)

    for pr in range(2):
        for rb in range(8):
            rs = slice(rb * 64, (rb + 1) * 64)
            p0, p1, p2 = (acc[2 * pr, rs, n * HD : (n + 1) * HD] for n in range(3))
            q0, q1, q2 = (acc[2 * pr + 1, rs, n * HD : (n + 1) * HD] for n in range(3))
            sp1, sp2, sq0, sq1 = swap(p1), swap(p2), swap(q0), swap(q1)
            tiles = (
                (p0, jnp.where(low, p1, sq0), jnp.where(low, sq0, sq1)),
                (jnp.where(low, sp1, sp2), jnp.where(low, sp2, q1), q2),
            )
            for j in range(2):
                for n in range(3):
                    at = j * 768 + pr * 384 + n * HD
                    out[rs, at : at + HD] = tiles[j][n].astype(BF16)

    for cp in sends:
        cp.wait_send()
    for d in range(1, 8):
        @pl.when(z + d < 8)
        def _():
            z_state(d).wait_send()
    for way in range(2):
        for n in range(2):
            for step in range(4 if way == n else 3):
                z_copy(way, z, n, step).wait_send()
    for zs in range(8):
        @pl.when(zs // 2 != y)
        def _():
            for n in range(2):
                y_copy(zs, n).wait_send()
    for j in range(2):
        for way in range(2):
            x_copy(way, urgent[way], j).wait_send()
            for n in range(2):
                x_copy(way, common[way][n], j).wait_send()
            relay_copy(way, j).wait_send()
        for i in range(4):
            for which in range(4):
                pair_copy(which, i, j).wait_send()
            zpair_copy(i, j).wait_send()
    for n in range(4):
        h_up(n).wait_send()
        h_dn(n).wait_send()
        h_relay(n).wait_send()


def body(
    query_rows, key_rows, value_rows, gate_rows, init_state, decay_rate, norm_gain, out_weight
):
    vm = pl.BlockSpec(memory_space=pltpu.VMEM)
    anyspace = pl.BlockSpec(memory_space=pl.ANY)
    dma = pltpu.SemaphoreType.DMA
    return pl.pallas_call(
        kernel,
        out_shape=jax.ShapeDtypeStruct((ROWS, 1536), BF16),
        in_specs=[pl.BlockSpec(memory_space=pltpu.SMEM), vm] + [anyspace] * 6,
        out_specs=vm,
        scratch_shapes=[
            pltpu.VMEM((ROWS, NH * HD), BF16),
            pltpu.VMEM((ROWS, NH * HD), BF16),
            pltpu.VMEM((ROWS, NH * HD), BF16),
            pltpu.VMEM((ROWS, NH * HD), BF16),
            pltpu.VMEM((ROWS, NH * HD), F32),
            pltpu.VMEM((ROWS, NH * HD), F32),
            pltpu.VMEM((NH, HD, HD), BF16),
            pltpu.VMEM((NH, HD, HD), BF16),
            pltpu.VMEM((8, HD, HD), BF16),
            pltpu.VMEM((8, HD, HD), F32),
            pltpu.VMEM((HD, HD), BF16),
            pltpu.VMEM((8, HD, HD), BF16),
            pltpu.VMEM((HD, HD), F32),
            pltpu.VMEM((NH, HD, HD), BF16),
            pltpu.VMEM((8, 96, 1024), BF16),
            pltpu.VMEM((4, 4, 2, 2, 96, 1024), BF16),
            pltpu.VMEM((4, ROWS, NH * HD), BF16),
            pltpu.VMEM((4, ROWS, 384), F32),
            dma((6,)), dma((7,)), dma((8,)), dma((7,)), dma((8,)), dma((7,)), dma((8,)),
            dma((2, 4, 2)), dma((2, 4, 2)), dma((8, 2)), dma((4, 2, 2)),
            dma((2, 2, 4)), dma((2, 2, 4)), dma((2, 2)), dma((2, 2)), dma((2, 4)), dma((2, 4)),
            dma((4, 2, 4)), dma((4, 2, 4)),
            dma((4,)), dma((4,)), dma((4,)), dma((4,)), dma((4,)), dma((4,)),
        ],
        compiler_params=pltpu.CompilerParams(
            collective_id=0, has_side_effects=True, vmem_limit_bytes=60 * 2**20
        ),
        cost_estimate=pl.CostEstimate(
            flops=8 * 10**9, bytes_accessed=6 * 2**20, transcendentals=10**6
        ),
    )(
        decay_rate, norm_gain[None, :], init_state, query_rows, key_rows, value_rows, gate_rows,
        out_weight.T,
    )


def solution(mesh):
    return jax.shard_map(
        body,
        mesh=mesh,
        in_specs=(
            P("ctx", "head"),
            P("ctx", "head"),
            P("ctx", "head"),
            P("ctx", "head"),
            P("head", None, None),
            P("head"),
            P("head"),
            P("head", "ctx"),
        ),
        out_specs=P("ctx", "head"),
        check_vma=False,
    )
```

```python
import jax
import jax.numpy as jnp
from jax import lax
from jax.sharding import PartitionSpec as P
from jax.experimental import pallas as pl
from jax.experimental.pallas import tpu as pltpu

MESH = pl.DeviceIdType.MESH
F32 = jnp.float32
BF16 = jnp.bfloat16
HD = 128
BLK = 256
ROWS = 512
NH = 8


def dot(a, b, ca=1, cb=0):
    return lax.dot_general(a, b, (((ca,), (cb,)), ((), ())), preferred_element_type=F32)

ORD = (0, 1, 3, 2)


def kernel(
    rate, gain, init, q_hbm, k_hbm, v_hbm, g_hbm, w_hbm, out,
    q, k, v, g, u, gs, c0, loc, rx1, exc, tx2, rx2, tx3, rx3, zb, wt, hidg, acc,
    lsem, s1, r1, s2, r2, s3, r3,
    sz, rz, sy, ry, sx, rx, srl, rrl, szp, rzp, s2d, r2d,
    shu, rhu, shd, rhd, shr, rhr,
):
    c = lax.axis_index("ctx")
    y = lax.axis_index("head")
    z = c // 8
    me = c % 8
    x = me // 2
    core = me % 2
    par = z % 2
    xup, xdn, xop = (x + 1) % 4, (x + 3) % 4, (x + 2) % 4

    def dev(zz, xx, yy, cc=core):
        return (zz * 8 + xx * 2 + cc, yy)

    def rcopy(src, dst, ss, rs, to):
        return pltpu.make_async_remote_copy(
            src_ref=src, dst_ref=dst, send_sem=ss, recv_sem=rs, device_id=to, device_id_type=MESH
        )

    barrier = pltpu.get_barrier_semaphore()
    for d in range(1, 8):
        pl.semaphore_signal(
            barrier, inc=1, device_id=(z * 8 + (me + d) % 8, y), device_id_type=MESH
        )
        pl.semaphore_signal(
            barrier, inc=1, device_id=(((z + d) % 8) * 8 + me, y), device_id_type=MESH
        )
    for d in range(1, 4):
        pl.semaphore_signal(barrier, inc=1, device_id=(c, (y + d) % 4), device_id_type=MESH)
    loads = [
        pltpu.make_async_copy(a, b, lsem.at[i])
        for i, (a, b) in enumerate(
            (
                (k_hbm, k), (v_hbm, v), (w_hbm, zb.at[z]), (q_hbm, q), (g_hbm, g),
                (init.at[me], tx3),
            )
        )
    ]
    for cp in loads:
        cp.start()

    def half(n):
        return pl.ds(48 * n, 48)

    def z_copy(way, zs, n, s):
        p = zb.at[zs, half(n)]
        to = dev((z + 1) % 8 if way == 0 else (z + 7) % 8, x, y)
        return rcopy(p, p, sz.at[way, s, n], rz.at[way, s, n], to)

    def z_start():
        for n in range(2):
            for way in range(2):
                z_copy(way, z, n, 0).start()
            y_send(z, n, 0)

    def y_copy(zs, n):
        return rcopy(
            zb.at[zs, half(n)], wt.at[y, x, zs % 2, core, half(n)],
            sy.at[zs, n], ry.at[y, zs % 2, n], dev(z, x, zs // 2),
        )

    def y_send(zs, n, s):
        rel = (y + 4 - zs // 2) % 4
        if s % 2 == 1:
            @pl.when(rel == 0)
            def _():
                pltpu.make_async_copy(
                    zb.at[zs, half(n)], wt.at[y, x, zs % 2, core, half(n)], ry.at[y, zs % 2, n]
                ).start()

        @pl.when((rel == 1) if s % 2 == 1 else (rel >= 2))
        def _():
            y_copy(zs, n).start()

    def z_event(s, n):
        for way in range(2):
            if s == 4 and way != n:
                continue
            zs = (z + 8 - s) % 8 if way == 0 else (z + s) % 8
            z_copy(way, zs, n, s - 1).wait_recv()
            if s < 3 or (s == 3 and way == n):
                z_copy(way, zs, n, s).start()
            y_send(zs, n, s)

    def dist(j):
        d = (2 * y + j + 8 - z) % 8
        return jnp.minimum(d, 8 - d)

    odd, even = 1 - par, par

    def order_at(i):
        if isinstance(i, int):
            return ORD[i]
        return jnp.where(i == 3, 2, jnp.where(i == 2, 3, i))

    def piece(i, quarter, j):
        return wt.at[(y + order_at(i)) % 4, quarter, j, core]

    def mine(m, j):
        return m + (0 if j is odd else 2 if j is even else 2 * ((par + j + 1) % 2))

    def other(m, j):
        return m + (2 if j is odd else 0 if j is even else 2 * ((par + j) % 2))

    beside = (z + 1 - 2 * par, (z + 7 + 2 * par) % 8)
    toward, source = (xup, xdn), (xdn, xup)

    def x_copy(way, i, j):
        p = piece(i, x, j)
        return rcopy(p, p, sx.at[way, j, i], rx.at[way, j, i], dev(z, toward[way], y))

    def pair_copy(which, i, j):
        p = piece(i, (x, xdn, xup, xop)[which], j)
        return rcopy(p, p, s2d.at[which, j, i], r2d.at[which, j, i], dev(z, x, y, 1 - core))

    def pair_wait(i):
        for which in range(4):
            for j in range(2):
                pair_copy(which, i, j).wait_recv()

    def relay_copy(way, j, own=True):
        i = mine(way, j) if own else other(way, j)
        p = piece(i, source[way], j)
        return rcopy(p, p, srl.at[j, i], rrl.at[j, i], dev(z, toward[way], y))

    def zn_copy(w, m, j):
        p = piece(mine(m, j), (xdn, xup, x)[w], j)
        return rcopy(p, p, szp.at[j, w, m], rzp.at[j, w, m], dev(beside[(w + m) % 2], x, y))

    def ready(i, j):
        yy = (y + order_at(i)) % 4
        for n in range(2):
            rcopy(
                zb.at[0, half(n)], wt.at[yy, x, j, core, half(n)], sy.at[0, n],
                ry.at[yy, j, n], dev(z, x, (y + 1) % 4),
            ).wait_recv()

    def x_early(s):
        @pl.when(dist(odd) == s)
        def _():
            ready(0, odd)
            for way in range(2):
                x_copy(way, 0, odd).start()
            zn_copy(2, 0, odd).start()
            pair_copy(0, 0, odd).start()

    def x_stage(s):
        j = odd if s % 2 == 1 else even

        @pl.when(dist(j) == s)
        def _():
            for m in range(s % 2, 2):
                ready(mine(m, j), j)
                for way in range(2):
                    x_copy(way, mine(m, j), j).start()
                zn_copy(2, m, j).start()
                pair_copy(0, mine(m, j), j).start()

    def x_event(j, m):
        for way in (m, 1 - m):
            x_copy(way, mine(m, j), j).wait_recv()
            if way == m:
                relay_copy(way, j).start()
            zn_copy(way, m, j).start()
            pair_copy(1 + way, mine(m, j), j).start()

    def opposite_event(j, way, own=True):
        relay_copy(way, j, own).wait_recv()
        pair_copy(3, mine(way, j) if own else other(way, j), j).start()

    def zn_event(w, m, j):
        zn_copy(w, m, j).wait_recv()
        if w == m:
            relay_copy(w, j, False).start()
        pair_copy((1, 2, 0)[w], other(m, j), j).start()

    yup, ydn, yop = (y + 1) % 4, (y + 3) % 4, (y + 2) % 4

    def chunk(who, n):
        return hidg.at[who, :, pl.ds(n * 256, 256)]

    def h_up(n):
        return rcopy(chunk(y, n), chunk(y, n), shu.at[n], rhu.at[n], dev(z, x, yup))

    def h_dn(n):
        return rcopy(chunk(y, n), chunk(y, n), shd.at[n], rhd.at[n], dev(z, x, ydn))

    def h_relay(n):
        who, to = (ydn, yup) if n < 2 else (yup, ydn)
        return rcopy(chunk(who, n), chunk(who, n), shr.at[n], rhr.at[n], dev(z, x, to))

    def h_relay_in(n):
        return rcopy(
            chunk(yop, n), chunk(yop, n), shr.at[n], rhr.at[n], dev(z, x, yup if n < 2 else ydn)
        )

    def h_event(n):
        h_up(n).wait_recv()
        if n < 2:
            h_relay(n).start()
        h_dn(n).wait_recv()
        if n >= 2:
            h_relay(n).start()

    def unit(who, quarter, start=False):
        t = dot(hidg[who], wt[who, quarter].reshape(384, 1024), 1, 1)
        acc[quarter] = t if start else acc[quarter] + t

    loads[0].wait()
    loads[1].wait()
    col = lax.broadcasted_iota(jnp.int32, (BLK, HD), 0).astype(F32)
    def contribs(h):
        r = rate[h]
        hs = slice(h * HD, (h + 1) * HD)
        kw = jnp.exp(-r * (BLK - 1.0 - col))
        k0 = (k[0:BLK, hs].astype(F32) * kw).astype(BF16)
        k1 = (k[BLK:ROWS, hs].astype(F32) * kw).astype(BF16)
        a0 = dot(k0, v[0:BLK, hs], 0, 0)
        a1 = dot(k1, v[BLK:ROWS, hs], 0, 0)
        c0[h] = a0.astype(BF16)
        loc[h] = (jnp.exp(jnp.full((1, HD), -r * BLK)) * a0 + a1).astype(BF16)

    for h in range(4):
        contribs(h)
    loads[2].wait()
    pl.semaphore_wait(barrier, 17)
    z_start()
    for h in range(4, NH):
        contribs(h)
    rx1[me] = loc[me]
    sends = []
    for d in range(1, 8):
        to = (me + d) % 8
        cp = rcopy(loc.at[to], rx1.at[me], s1.at[d - 1], r1.at[me], (z * 8 + to, y))
        cp.start()
        sends.append(cp)

    loads[3].wait()
    loads[4].wait()
    loads[5].wait()
    ii = lax.broadcasted_iota(jnp.int32, (BLK, BLK), 0)
    jj = lax.broadcasted_iota(jnp.int32, (BLK, BLK), 1)
    off = (ii - jj).astype(F32)

    def intra(h):
        r = rate[h]
        hs = slice(h * HD, (h + 1) * HD)
        decay = jnp.where(off >= 0.0, jnp.exp(-r * jnp.maximum(off, 0.0)), 0.0)
        for b in range(2):
            rs = slice(b * BLK, (b + 1) * BLK)
            w = (dot(q[rs, hs], k[rs, hs], 1, 1) * decay).astype(BF16)
            o = dot(w, v[rs, hs])
            if b == 1:
                o = o + jnp.exp(-r * (col + 1.0)) * dot(q[rs, hs], c0[h])
            u[rs, hs] = o
        gs[:, hs] = jax.nn.sigmoid(g[:, hs].astype(F32)) * gain[:, hs]

    intra(0)
    intra(1)
    z_event(1, 0)
    for d in range(1, 8):
        p = (me + 8 - d) % 8
        rcopy(loc.at[0], rx1.at[p], s1.at[0], r1.at[p], (z * 8 + p, y)).wait_recv()
    rm = rate[me]
    d512 = jnp.exp(jnp.full((1, HD), -rm * 512.0))
    e = jnp.zeros((HD, HD), F32)
    for p in range(8):
        exc[p] = e
        e = d512 * e + rx1[p].astype(F32)
    tx2[...] = e.astype(BF16)

    def z_state(d):
        return rcopy(tx2, rx2.at[z], s2.at[d - 1], r2.at[z], ((z + d) % 8 * 8 + me, y))

    for d in range(1, 8):
        @pl.when(z + d < 8)
        def _():
            z_state(d).start()

    z_event(1, 1)
    intra(2)
    intra(3)
    z_event(2, 0)
    intra(4)
    intra(5)
    z_event(2, 1)
    intra(6)
    intra(7)

    for i in range(7):
        @pl.when(i < z)
        def _():
            rcopy(tx2, rx2.at[i], s2.at[0], r2.at[i], (i * 8 + me, y)).wait_recv()
            tx3[...] = jnp.exp(jnp.full((1, HD), -rm * 4096.0)) * tx3[...] + rx2[i].astype(F32)
    base = tx3[...]
    for p in range(8):
        rx1[p] = (jnp.exp(jnp.full((1, HD), -rm * (512.0 * p))) * base + exc[p]).astype(BF16)
    rx3[me] = rx1[me]
    for d in range(1, 8):
        to = (me + d) % 8
        cp = rcopy(rx1.at[to], rx3.at[me], s3.at[d - 1], r3.at[me], (z * 8 + to, y))
        cp.start()
        sends.append(cp)

    x_early(1)
    z_event(3, 0)
    z_event(3, 1)
    x_early(3)
    z_event(4, 0)
    z_event(4, 1)

    row = lax.broadcasted_iota(jnp.int32, (ROWS, HD), 0).astype(F32)
    for h in range(NH):
        @pl.when(h != me)
        def _():
            rcopy(rx1.at[0], rx3.at[h], s3.at[0], r3.at[h], (z * 8 + h, y)).wait_recv()
        hs = slice(h * HD, (h + 1) * HD)
        at = u[:, hs] + jnp.exp(-rate[h] * (row + 1.0)) * dot(q[:, hs], rx3[h])
        scale = lax.rsqrt(jnp.mean(at * at, axis=-1, keepdims=True) + 1e-06)
        hidg[y, :, hs] = (at * scale * gs[:, hs]).astype(BF16)
        if h % 2 == 1:
            h_up(h // 2).start()
            h_dn(h // 2).start()

    x_stage(0)
    x_stage(1)
    x_event(odd, 0)
    x_stage(2)
    x_stage(3)
    x_stage(4)
    x_event(odd, 1)
    zn_event(2, 0, even)
    zn_event(0, 0, even)
    zn_event(1, 0, even)
    zn_event(2, 1, even)
    x_event(even, 0)
    zn_event(1, 1, even)
    zn_event(0, 1, even)
    x_event(even, 1)
    opposite_event(odd, 0)
    opposite_event(odd, 1)
    h_event(0)
    h_event(1)
    opposite_event(even, 0, False)
    zn_event(2, 0, odd)
    zn_event(0, 0, odd)
    zn_event(1, 0, odd)
    h_event(2)
    h_event(3)
    zn_event(2, 1, odd)
    zn_event(1, 1, odd)
    zn_event(0, 1, odd)
    opposite_event(even, 1, False)
    pair_wait(0)
    for quarter in (x, xdn, xup, xop):
        unit(y, quarter, True)
    pair_wait(1)
    for quarter in (x, xdn, xup, xop):
        unit(yup, quarter)
    opposite_event(even, 0)
    opposite_event(even, 1)
    opposite_event(odd, 0, False)
    opposite_event(odd, 1, False)
    pair_wait(2)
    for quarter in (x, xdn, xup, xop):
        unit(ydn, quarter)
    pair_wait(3)
    for n in range(4):
        h_relay_in(n).wait_recv()
    for quarter in (x, xdn, xup, xop):
        unit(yop, quarter)

    low = lax.broadcasted_iota(jnp.int32, (64, HD), 1) < 64

    def swap(t):
        return pltpu.roll(t, 64, axis=1)

    for pr in range(2):
        for rb in range(8):
            rs = slice(rb * 64, (rb + 1) * 64)
            p0, p1, p2 = (acc[2 * pr, rs, n * HD : (n + 1) * HD] for n in range(3))
            q0, q1, q2 = (acc[2 * pr + 1, rs, n * HD : (n + 1) * HD] for n in range(3))
            sp1, sp2, sq0, sq1 = swap(p1), swap(p2), swap(q0), swap(q1)
            tiles = (
                (p0, jnp.where(low, p1, sq0), jnp.where(low, sq0, sq1)),
                (jnp.where(low, sp1, sp2), jnp.where(low, sp2, q1), q2),
            )
            for j in range(2):
                for n in range(3):
                    at = j * 768 + pr * 384 + n * HD
                    out[rs, at : at + HD] = tiles[j][n].astype(BF16)

    for cp in sends:
        cp.wait_send()
    for d in range(1, 8):
        @pl.when(z + d < 8)
        def _():
            z_state(d).wait_send()
    for way in range(2):
        for n in range(2):
            for step in range(4 if way == n else 3):
                z_copy(way, z, n, step).wait_send()
    for zs in range(8):
        rel = (y + 4 - zs // 2) % 4
        far = (z + zs) % 2

        @pl.when(((far == 1) & (rel == 1)) | ((far == 0) & (rel >= 2)))
        def _():
            for n in range(2):
                y_copy(zs, n).wait_send()
    for j in range(2):
        for way in range(2):
            for m in range(2):
                x_copy(way, mine(m, j), j).wait_send()
            relay_copy(way, j).wait_send()
            relay_copy(way, j, False).wait_send()
            for w in range(3):
                zn_copy(w, way, j).wait_send()
        for i in range(4):
            for which in range(4):
                pair_copy(which, i, j).wait_send()
    for n in range(4):
        h_up(n).wait_send()
        h_dn(n).wait_send()
        h_relay(n).wait_send()


def body(
    query_rows, key_rows, value_rows, gate_rows, init_state, decay_rate, norm_gain, out_weight
):
    vm = pl.BlockSpec(memory_space=pltpu.VMEM)
    anyspace = pl.BlockSpec(memory_space=pl.ANY)
    dma = pltpu.SemaphoreType.DMA
    return pl.pallas_call(
        kernel,
        out_shape=jax.ShapeDtypeStruct((ROWS, 1536), BF16),
        in_specs=[pl.BlockSpec(memory_space=pltpu.SMEM), vm] + [anyspace] * 6,
        out_specs=vm,
        scratch_shapes=[
            pltpu.VMEM((ROWS, NH * HD), BF16),
            pltpu.VMEM((ROWS, NH * HD), BF16),
            pltpu.VMEM((ROWS, NH * HD), BF16),
            pltpu.VMEM((ROWS, NH * HD), BF16),
            pltpu.VMEM((ROWS, NH * HD), F32),
            pltpu.VMEM((ROWS, NH * HD), F32),
            pltpu.VMEM((NH, HD, HD), BF16),
            pltpu.VMEM((NH, HD, HD), BF16),
            pltpu.VMEM((8, HD, HD), BF16),
            pltpu.VMEM((8, HD, HD), F32),
            pltpu.VMEM((HD, HD), BF16),
            pltpu.VMEM((8, HD, HD), BF16),
            pltpu.VMEM((HD, HD), F32),
            pltpu.VMEM((NH, HD, HD), BF16),
            pltpu.VMEM((8, 96, 1024), BF16),
            pltpu.VMEM((4, 4, 2, 2, 96, 1024), BF16),
            pltpu.VMEM((4, ROWS, NH * HD), BF16),
            pltpu.VMEM((4, ROWS, 384), F32),
            dma((6,)), dma((7,)), dma((8,)), dma((7,)), dma((8,)), dma((7,)), dma((8,)),
            dma((2, 4, 2)), dma((2, 4, 2)), dma((8, 2)), dma((4, 2, 2)),
            dma((2, 2, 4)), dma((2, 2, 4)), dma((2, 4)), dma((2, 4)), dma((2, 3, 2)), dma((2, 3, 2)),
            dma((4, 2, 4)), dma((4, 2, 4)),
            dma((4,)), dma((4,)), dma((4,)), dma((4,)), dma((4,)), dma((4,)),
        ],
        compiler_params=pltpu.CompilerParams(
            collective_id=0, has_side_effects=True, vmem_limit_bytes=60 * 2**20
        ),
        cost_estimate=pl.CostEstimate(
            flops=8 * 10**9, bytes_accessed=6 * 2**20, transcendentals=10**6
        ),
    )(
        decay_rate, norm_gain[None, :], init_state, query_rows, key_rows, value_rows, gate_rows,
        out_weight.T,
    )


def solution(mesh):
    return jax.shard_map(
        body,
        mesh=mesh,
        in_specs=(
            P("ctx", "head"),
            P("ctx", "head"),
            P("ctx", "head"),
            P("ctx", "head"),
            P("head", None, None),
            P("head"),
            P("head"),
            P("head", "ctx"),
        ),
        out_specs=P("ctx", "head"),
        check_vma=False,
    )
```

```python
import jax
import jax.numpy as jnp
from jax import lax
from jax.sharding import PartitionSpec as P
from jax.experimental import pallas as pl
from jax.experimental.pallas import tpu as pltpu

MESH = pl.DeviceIdType.MESH
F32 = jnp.float32
BF16 = jnp.bfloat16
HD = 128
BLK = 256
ROWS = 512
NH = 8


def dot(a, b, ca=1, cb=0):
    return lax.dot_general(a, b, (((ca,), (cb,)), ((), ())), preferred_element_type=F32)

ORD = (0, 1, 3, 2)


def kernel(
    rate, gain, init, q_hbm, k_hbm, v_hbm, g_hbm, w_hbm, out,
    q, k, v, g, u, gs, c0, loc, rx1, exc, tx2, rx2, tx3, rx3, zb, wt, hidg, acc, res,
    lsem, s1, r1, s2, r2, s3, r3,
    sz, rz, sy, ry, sx, rx, srl, rrl, szp, rzp, s2d, r2d,
    shu, rhu, shd, rhd, shr, rhr, osem,
):
    c = lax.axis_index("ctx")
    y = lax.axis_index("head")
    z = c // 8
    me = c % 8
    x = me // 2
    core = me % 2
    par = z % 2
    xup, xdn, xop = (x + 1) % 4, (x + 3) % 4, (x + 2) % 4

    def dev(zz, xx, yy, cc=core):
        return (zz * 8 + xx * 2 + cc, yy)

    def rcopy(src, dst, ss, rs, to):
        return pltpu.make_async_remote_copy(
            src_ref=src, dst_ref=dst, send_sem=ss, recv_sem=rs, device_id=to, device_id_type=MESH
        )

    barrier = pltpu.get_barrier_semaphore()
    for d in range(1, 8):
        pl.semaphore_signal(
            barrier, inc=1, device_id=(z * 8 + (me + d) % 8, y), device_id_type=MESH
        )
        pl.semaphore_signal(
            barrier, inc=1, device_id=(((z + d) % 8) * 8 + me, y), device_id_type=MESH
        )
    for d in range(1, 4):
        pl.semaphore_signal(barrier, inc=1, device_id=(c, (y + d) % 4), device_id_type=MESH)
    loads = [
        pltpu.make_async_copy(a, b, lsem.at[i])
        for i, (a, b) in enumerate(
            (
                (k_hbm, k), (v_hbm, v), (w_hbm, zb.at[z]), (q_hbm, q), (g_hbm, g),
                (init.at[me], tx3),
            )
        )
    ]
    for cp in loads:
        cp.start()

    def half(n):
        return pl.ds(48 * n, 48)

    def z_copy(way, zs, n, s):
        p = zb.at[zs, half(n)]
        to = dev((z + 1) % 8 if way == 0 else (z + 7) % 8, x, y)
        return rcopy(p, p, sz.at[way, s, n], rz.at[way, s, n], to)

    def z_start():
        for n in range(2):
            for way in range(2):
                z_copy(way, z, n, 0).start()
            y_send(z, n, 0)

    def y_copy(zs, n):
        return rcopy(
            zb.at[zs, half(n)], wt.at[y, x, zs % 2, core, half(n)],
            sy.at[zs, n], ry.at[y, zs % 2, n], dev(z, x, zs // 2),
        )

    def y_send(zs, n, s):
        rel = (y + 4 - zs // 2) % 4
        if s % 2 == 1:
            @pl.when(rel == 0)
            def _():
                pltpu.make_async_copy(
                    zb.at[zs, half(n)], wt.at[y, x, zs % 2, core, half(n)], ry.at[y, zs % 2, n]
                ).start()

        @pl.when((rel == 1) if s % 2 == 1 else (rel >= 2))
        def _():
            y_copy(zs, n).start()

    def z_event(s, n):
        for way in range(2):
            if s == 4 and way != n:
                continue
            zs = (z + 8 - s) % 8 if way == 0 else (z + s) % 8
            z_copy(way, zs, n, s - 1).wait_recv()
            if s < 3 or (s == 3 and way == n):
                z_copy(way, zs, n, s).start()
            y_send(zs, n, s)

    def dist(j):
        d = (2 * y + j + 8 - z) % 8
        return jnp.minimum(d, 8 - d)

    odd, even = 1 - par, par

    def order_at(i):
        if isinstance(i, int):
            return ORD[i]
        return jnp.where(i == 3, 2, jnp.where(i == 2, 3, i))

    def piece(i, quarter, j):
        return wt.at[(y + order_at(i)) % 4, quarter, j, core]

    def mine(m, j):
        return m + (0 if j is odd else 2 if j is even else 2 * ((par + j + 1) % 2))

    def other(m, j):
        return m + (2 if j is odd else 0 if j is even else 2 * ((par + j) % 2))

    beside = (z + 1 - 2 * par, (z + 7 + 2 * par) % 8)
    toward, source = (xup, xdn), (xdn, xup)

    def x_copy(way, i, j):
        p = piece(i, x, j)
        return rcopy(p, p, sx.at[way, j, i], rx.at[way, j, i], dev(z, toward[way], y))

    def pair_copy(which, i, j):
        p = piece(i, (x, xdn, xup, xop)[which], j)
        return rcopy(p, p, s2d.at[which, j, i], r2d.at[which, j, i], dev(z, x, y, 1 - core))

    def need(which, i):
        for j in range(2):
            pair_copy(which, i, j).wait_recv()

    def relay_copy(way, j, own=True):
        i = mine(way, j) if own else other(way, j)
        p = piece(i, source[way], j)
        return rcopy(p, p, srl.at[j, i], rrl.at[j, i], dev(z, toward[way], y))

    def zn_copy(w, m, j):
        p = piece(mine(m, j), (xdn, xup, x)[w], j)
        return rcopy(p, p, szp.at[j, w, m], rzp.at[j, w, m], dev(beside[(w + m) % 2], x, y))

    def ready(i, j):
        yy = (y + order_at(i)) % 4
        for n in range(2):
            rcopy(
                zb.at[0, half(n)], wt.at[yy, x, j, core, half(n)], sy.at[0, n],
                ry.at[yy, j, n], dev(z, x, (y + 1) % 4),
            ).wait_recv()

    def x_early(s):
        @pl.when(dist(odd) == s)
        def _():
            ready(0, odd)
            for way in range(2):
                x_copy(way, 0, odd).start()
            zn_copy(2, 0, odd).start()
            pair_copy(0, 0, odd).start()

    def x_stage(s):
        j = odd if s % 2 == 1 else even

        @pl.when(dist(j) == s)
        def _():
            for m in range(s % 2, 2):
                ready(mine(m, j), j)
                for way in range(2):
                    x_copy(way, mine(m, j), j).start()
                zn_copy(2, m, j).start()
                pair_copy(0, mine(m, j), j).start()

    def x_event(j, m):
        for way in (m, 1 - m):
            x_copy(way, mine(m, j), j).wait_recv()
            if way == m:
                relay_copy(way, j).start()
            zn_copy(way, m, j).start()
            pair_copy(1 + way, mine(m, j), j).start()

    def opposite_event(j, way, own=True):
        relay_copy(way, j, own).wait_recv()
        pair_copy(3, mine(way, j) if own else other(way, j), j).start()

    def zn_event(w, m, j):
        zn_copy(w, m, j).wait_recv()
        if w == m:
            relay_copy(w, j, False).start()
        pair_copy((1, 2, 0)[w], other(m, j), j).start()

    yup, ydn, yop = (y + 1) % 4, (y + 3) % 4, (y + 2) % 4

    def chunk(who, n):
        return hidg.at[who, :, pl.ds(n * 256, 256)]

    def h_up(n):
        return rcopy(chunk(y, n), chunk(y, n), shu.at[n], rhu.at[n], dev(z, x, yup))

    def h_dn(n):
        return rcopy(chunk(y, n), chunk(y, n), shd.at[n], rhd.at[n], dev(z, x, ydn))

    def h_relay(n):
        who, to = (ydn, yup) if n < 2 else (yup, ydn)
        return rcopy(chunk(who, n), chunk(who, n), shr.at[n], rhr.at[n], dev(z, x, to))

    def h_relay_in(n):
        return rcopy(
            chunk(yop, n), chunk(yop, n), shr.at[n], rhr.at[n], dev(z, x, yup if n < 2 else ydn)
        )

    def h_event(n):
        h_up(n).wait_recv()
        if n < 2:
            h_relay(n).start()
        h_dn(n).wait_recv()
        if n >= 2:
            h_relay(n).start()

    def unit(who, quarter, start=False):
        t = dot(hidg[who], wt[who, quarter].reshape(384, 1024), 1, 1)
        acc[quarter] = t if start else acc[quarter] + t

    loads[0].wait()
    loads[1].wait()
    col = lax.broadcasted_iota(jnp.int32, (BLK, HD), 0).astype(F32)
    def contribs(h):
        r = rate[h]
        hs = slice(h * HD, (h + 1) * HD)
        kw = jnp.exp(-r * (BLK - 1.0 - col))
        k0 = (k[0:BLK, hs].astype(F32) * kw).astype(BF16)
        k1 = (k[BLK:ROWS, hs].astype(F32) * kw).astype(BF16)
        a0 = dot(k0, v[0:BLK, hs], 0, 0)
        a1 = dot(k1, v[BLK:ROWS, hs], 0, 0)
        c0[h] = a0.astype(BF16)
        loc[h] = (jnp.exp(jnp.full((1, HD), -r * BLK)) * a0 + a1).astype(BF16)

    for h in range(4):
        contribs(h)
    loads[2].wait()
    pl.semaphore_wait(barrier, 17)
    z_start()
    for h in range(4, NH):
        contribs(h)
    rx1[me] = loc[me]
    sends = []
    for d in range(1, 8):
        to = (me + d) % 8
        cp = rcopy(loc.at[to], rx1.at[me], s1.at[d - 1], r1.at[me], (z * 8 + to, y))
        cp.start()
        sends.append(cp)

    loads[3].wait()
    loads[4].wait()
    loads[5].wait()
    ii = lax.broadcasted_iota(jnp.int32, (BLK, BLK), 0)
    jj = lax.broadcasted_iota(jnp.int32, (BLK, BLK), 1)
    off = (ii - jj).astype(F32)

    def intra(h):
        r = rate[h]
        hs = slice(h * HD, (h + 1) * HD)
        decay = jnp.where(off >= 0.0, jnp.exp(-r * jnp.maximum(off, 0.0)), 0.0)
        for b in range(2):
            rs = slice(b * BLK, (b + 1) * BLK)
            w = (dot(q[rs, hs], k[rs, hs], 1, 1) * decay).astype(BF16)
            o = dot(w, v[rs, hs])
            if b == 1:
                o = o + jnp.exp(-r * (col + 1.0)) * dot(q[rs, hs], c0[h])
            u[rs, hs] = o
        gs[:, hs] = jax.nn.sigmoid(g[:, hs].astype(F32)) * gain[:, hs]

    intra(0)
    intra(1)
    z_event(1, 0)
    for d in range(1, 8):
        p = (me + 8 - d) % 8
        rcopy(loc.at[0], rx1.at[p], s1.at[0], r1.at[p], (z * 8 + p, y)).wait_recv()
    rm = rate[me]
    d512 = jnp.exp(jnp.full((1, HD), -rm * 512.0))
    e = jnp.zeros((HD, HD), F32)
    for p in range(8):
        exc[p] = e
        e = d512 * e + rx1[p].astype(F32)
    tx2[...] = e.astype(BF16)

    def z_state(d):
        return rcopy(tx2, rx2.at[z], s2.at[d - 1], r2.at[z], ((z + d) % 8 * 8 + me, y))

    for d in range(1, 8):
        @pl.when(z + d < 8)
        def _():
            z_state(d).start()

    z_event(1, 1)
    intra(2)
    intra(3)
    z_event(2, 0)
    intra(4)
    intra(5)
    z_event(2, 1)
    intra(6)
    intra(7)

    for i in range(7):
        @pl.when(i < z)
        def _():
            rcopy(tx2, rx2.at[i], s2.at[0], r2.at[i], (i * 8 + me, y)).wait_recv()
            tx3[...] = jnp.exp(jnp.full((1, HD), -rm * 4096.0)) * tx3[...] + rx2[i].astype(F32)
    base = tx3[...]
    for p in range(8):
        rx1[p] = (jnp.exp(jnp.full((1, HD), -rm * (512.0 * p))) * base + exc[p]).astype(BF16)
    rx3[me] = rx1[me]
    for d in range(1, 8):
        to = (me + d) % 8
        cp = rcopy(rx1.at[to], rx3.at[me], s3.at[d - 1], r3.at[me], (z * 8 + to, y))
        cp.start()
        sends.append(cp)

    x_early(1)
    z_event(3, 0)
    z_event(3, 1)
    x_early(3)

    row = lax.broadcasted_iota(jnp.int32, (ROWS, HD), 0).astype(F32)
    for h in range(NH):
        @pl.when(h != me)
        def _():
            rcopy(rx1.at[0], rx3.at[h], s3.at[0], r3.at[h], (z * 8 + h, y)).wait_recv()
        hs = slice(h * HD, (h + 1) * HD)
        at = u[:, hs] + jnp.exp(-rate[h] * (row + 1.0)) * dot(q[:, hs], rx3[h])
        scale = lax.rsqrt(jnp.mean(at * at, axis=-1, keepdims=True) + 1e-06)
        hidg[y, :, hs] = (at * scale * gs[:, hs]).astype(BF16)
        if h == 7:
            z_event(4, 0)
            z_event(4, 1)
            for n in range(4):
                h_up(n).start()
                h_dn(n).start()

    x_stage(0)
    x_stage(1)
    x_event(odd, 0)
    x_stage(2)
    x_stage(3)
    x_stage(4)
    def units(i, which):
        for n in which:
            need(n, i)
            unit((y, yup, ydn, yop)[i], (x, xdn, xup, xop)[n], i == 0)

    x_event(odd, 1)
    zn_event(2, 0, even)
    zn_event(0, 0, even)
    zn_event(1, 0, even)
    zn_event(2, 1, even)
    x_event(even, 0)
    zn_event(1, 1, even)
    zn_event(0, 1, even)
    x_event(even, 1)
    units(0, (0, 1, 2))
    h_event(0)
    h_event(1)
    zn_event(2, 0, odd)
    zn_event(0, 0, odd)
    zn_event(1, 0, odd)
    h_event(2)
    zn_event(2, 1, odd)
    zn_event(1, 1, odd)
    zn_event(0, 1, odd)
    h_event(3)
    opposite_event(odd, 0)
    opposite_event(odd, 1)
    opposite_event(even, 0, False)
    opposite_event(even, 1, False)
    units(1, (0, 1, 2))
    opposite_event(even, 0)
    opposite_event(even, 1)
    units(0, (3,))
    units(1, (3,))
    opposite_event(odd, 0, False)
    units(2, (0, 1, 2))
    opposite_event(odd, 1, False)
    units(2, (3,))
    for n in range(3):
        need(n, 3)
    def part(quarter, n):
        ks = slice(n * 256, (n + 1) * 256)
        return dot(hidg[yop, :, ks], wt[yop, quarter, :, :, :, ks].reshape(384, 256), 1, 1)

    h_relay_in(0).wait_recv()
    h_relay_in(2).wait_recv()
    for n, quarter in enumerate((x, xdn, xup, xop)):
        if n == 3:
            need(3, 3)
        acc[quarter] += part(quarter, 0) + part(quarter, 2)
    h_relay_in(1).wait_recv()
    h_relay_in(3).wait_recv()
    for n, quarter in enumerate((x, xdn, xup, xop)):
        res[quarter] = (acc[quarter] + part(quarter, 1) + part(quarter, 3)).astype(BF16)
        pltpu.make_async_copy(res.at[quarter], out.at[quarter], osem.at[n]).start()
    for n, quarter in enumerate((x, xdn, xup, xop)):
        pltpu.make_async_copy(res.at[quarter], out.at[quarter], osem.at[n]).wait()
    for cp in sends:
        cp.wait_send()
    for d in range(1, 8):
        @pl.when(z + d < 8)
        def _():
            z_state(d).wait_send()
    for way in range(2):
        for n in range(2):
            for step in range(4 if way == n else 3):
                z_copy(way, z, n, step).wait_send()
    for zs in range(8):
        rel = (y + 4 - zs // 2) % 4
        far = (z + zs) % 2

        @pl.when(((far == 1) & (rel == 1)) | ((far == 0) & (rel >= 2)))
        def _():
            for n in range(2):
                y_copy(zs, n).wait_send()
    for j in range(2):
        for way in range(2):
            for m in range(2):
                x_copy(way, mine(m, j), j).wait_send()
            relay_copy(way, j).wait_send()
            relay_copy(way, j, False).wait_send()
            for w in range(3):
                zn_copy(w, way, j).wait_send()
        for i in range(4):
            for which in range(4):
                pair_copy(which, i, j).wait_send()
    for n in range(4):
        h_up(n).wait_send()
        h_dn(n).wait_send()
        h_relay(n).wait_send()


def assemble(quarters, out):
    low = lax.broadcasted_iota(jnp.int32, (64, HD), 1) < 64

    def swap(t):
        return pltpu.roll(t, 64, axis=1)

    for pr in range(2):
        for rb in range(8):
            rs = slice(rb * 64, (rb + 1) * 64)
            p0, p1, p2 = (
                quarters[2 * pr, rs, n * HD : (n + 1) * HD].astype(F32) for n in range(3)
            )
            q0, q1, q2 = (
                quarters[2 * pr + 1, rs, n * HD : (n + 1) * HD].astype(F32) for n in range(3)
            )
            sp1, sp2, sq0, sq1 = swap(p1), swap(p2), swap(q0), swap(q1)
            tiles = (
                (p0, jnp.where(low, p1, sq0), jnp.where(low, sq0, sq1)),
                (jnp.where(low, sp1, sp2), jnp.where(low, sp2, q1), q2),
            )
            for j in range(2):
                for n in range(3):
                    at = j * 768 + pr * 384 + n * HD
                    out[rs, at : at + HD] = tiles[j][n].astype(BF16)


def body(
    query_rows, key_rows, value_rows, gate_rows, init_state, decay_rate, norm_gain, out_weight
):
    vm = pl.BlockSpec(memory_space=pltpu.VMEM)
    anyspace = pl.BlockSpec(memory_space=pl.ANY)
    dma = pltpu.SemaphoreType.DMA
    quarters = pl.pallas_call(
        kernel,
        out_shape=jax.ShapeDtypeStruct((4, ROWS, 384), BF16),
        in_specs=[pl.BlockSpec(memory_space=pltpu.SMEM), vm] + [anyspace] * 6,
        out_specs=anyspace,
        scratch_shapes=[
            pltpu.VMEM((ROWS, NH * HD), BF16),
            pltpu.VMEM((ROWS, NH * HD), BF16),
            pltpu.VMEM((ROWS, NH * HD), BF16),
            pltpu.VMEM((ROWS, NH * HD), BF16),
            pltpu.VMEM((ROWS, NH * HD), F32),
            pltpu.VMEM((ROWS, NH * HD), F32),
            pltpu.VMEM((NH, HD, HD), BF16),
            pltpu.VMEM((NH, HD, HD), BF16),
            pltpu.VMEM((8, HD, HD), BF16),
            pltpu.VMEM((8, HD, HD), F32),
            pltpu.VMEM((HD, HD), BF16),
            pltpu.VMEM((8, HD, HD), BF16),
            pltpu.VMEM((HD, HD), F32),
            pltpu.VMEM((NH, HD, HD), BF16),
            pltpu.VMEM((8, 96, 1024), BF16),
            pltpu.VMEM((4, 4, 2, 2, 96, 1024), BF16),
            pltpu.VMEM((4, ROWS, NH * HD), BF16),
            pltpu.VMEM((4, ROWS, 384), F32),
            pltpu.VMEM((4, ROWS, 384), BF16),
            dma((6,)), dma((7,)), dma((8,)), dma((7,)), dma((8,)), dma((7,)), dma((8,)),
            dma((2, 4, 2)), dma((2, 4, 2)), dma((8, 2)), dma((4, 2, 2)),
            dma((2, 2, 4)), dma((2, 2, 4)), dma((2, 4)), dma((2, 4)), dma((2, 3, 2)), dma((2, 3, 2)),
            dma((4, 2, 4)), dma((4, 2, 4)),
            dma((4,)), dma((4,)), dma((4,)), dma((4,)), dma((4,)), dma((4,)), dma((4,)),
        ],
        compiler_params=pltpu.CompilerParams(
            collective_id=0, has_side_effects=True, vmem_limit_bytes=60 * 2**20
        ),
        cost_estimate=pl.CostEstimate(
            flops=8 * 10**9, bytes_accessed=6 * 2**20, transcendentals=10**6
        ),
    )(
        decay_rate, norm_gain[None, :], init_state, query_rows, key_rows, value_rows, gate_rows,
        out_weight.T,
    )
    return pl.pallas_call(
        assemble,
        out_shape=jax.ShapeDtypeStruct((ROWS, 1536), BF16),
        in_specs=[vm],
        out_specs=vm,
    )(quarters)


def solution(mesh):
    return jax.shard_map(
        body,
        mesh=mesh,
        in_specs=(
            P("ctx", "head"),
            P("ctx", "head"),
            P("ctx", "head"),
            P("ctx", "head"),
            P("head", None, None),
            P("head"),
            P("head"),
            P("head", "ctx"),
        ),
        out_specs=P("ctx", "head"),
        check_vma=False,
    )
```

```python
import jax
import jax.numpy as jnp
from jax import lax
from jax.sharding import PartitionSpec as P
from jax.experimental import pallas as pl
from jax.experimental.pallas import tpu as pltpu

MESH = pl.DeviceIdType.MESH
F32 = jnp.float32
BF16 = jnp.bfloat16
HD = 128
BLK = 256
ROWS = 512
NH = 8


def dot(a, b, ca=1, cb=0):
    return lax.dot_general(a, b, (((ca,), (cb,)), ((), ())), preferred_element_type=F32)

ORD = (0, 1, 3, 2)


def kernel(
    rate, gain, init, q_hbm, k_hbm, v_hbm, g_hbm, w_hbm, out,
    q, k, v, g, u, gs, c0, loc, rx1, exc, tx2, rx2, tx3, rx3, zb, wt, hidg, acc, res,
    lsem, s1, r1, s2, r2, s3, r3,
    sz, rz, sy, ry, sx, rx, srl, rrl, szp, rzp, s2d, r2d,
    shu, rhu, shd, rhd, shr, rhr, osem,
):
    c = lax.axis_index("ctx")
    y = lax.axis_index("head")
    z = c // 8
    me = c % 8
    x = me // 2
    core = me % 2
    par = z % 2
    xup, xdn, xop = (x + 1) % 4, (x + 3) % 4, (x + 2) % 4

    def dev(zz, xx, yy, cc=core):
        return (zz * 8 + xx * 2 + cc, yy)

    def rcopy(src, dst, ss, rs, to):
        return pltpu.make_async_remote_copy(
            src_ref=src, dst_ref=dst, send_sem=ss, recv_sem=rs, device_id=to, device_id_type=MESH
        )

    barrier = pltpu.get_barrier_semaphore()
    for d in range(1, 8):
        pl.semaphore_signal(
            barrier, inc=1, device_id=(z * 8 + (me + d) % 8, y), device_id_type=MESH
        )
        pl.semaphore_signal(
            barrier, inc=1, device_id=(((z + d) % 8) * 8 + me, y), device_id_type=MESH
        )
    for d in range(1, 4):
        pl.semaphore_signal(barrier, inc=1, device_id=(c, (y + d) % 4), device_id_type=MESH)
    loads = [
        pltpu.make_async_copy(a, b, lsem.at[i])
        for i, (a, b) in enumerate(
            (
                (k_hbm, k), (v_hbm, v), (w_hbm, zb.at[z]), (q_hbm, q), (g_hbm, g),
                (init.at[me], tx3),
            )
        )
    ]
    for cp in loads:
        cp.start()

    def half(n):
        return pl.ds(48 * n, 48)

    def z_copy(way, zs, n, s):
        p = zb.at[zs, half(n)]
        to = dev((z + 1) % 8 if way == 0 else (z + 7) % 8, x, y)
        return rcopy(p, p, sz.at[way, s, n], rz.at[way, s, n], to)

    def z_start():
        for n in range(2):
            for way in range(2):
                z_copy(way, z, n, 0).start()
            y_send(z, n, 0)

    def y_copy(zs, n):
        return rcopy(
            zb.at[zs, half(n)], wt.at[y, x, zs % 2, core, half(n)],
            sy.at[zs, n], ry.at[y, zs % 2, n], dev(z, x, zs // 2),
        )

    def y_send(zs, n, s):
        rel = (y + 4 - zs // 2) % 4
        if s % 2 == 1:
            @pl.when(rel == 0)
            def _():
                pltpu.make_async_copy(
                    zb.at[zs, half(n)], wt.at[y, x, zs % 2, core, half(n)], ry.at[y, zs % 2, n]
                ).start()

        @pl.when((rel == 1) if s % 2 == 1 else (rel >= 2))
        def _():
            y_copy(zs, n).start()

    def z_event(s, n):
        for way in range(2):
            if s == 4 and way != n:
                continue
            zs = (z + 8 - s) % 8 if way == 0 else (z + s) % 8
            z_copy(way, zs, n, s - 1).wait_recv()
            if s < 3 or (s == 3 and way == n):
                z_copy(way, zs, n, s).start()
            y_send(zs, n, s)

    def dist(j):
        d = (2 * y + j + 8 - z) % 8
        return jnp.minimum(d, 8 - d)

    odd, even = 1 - par, par

    def order_at(i):
        if isinstance(i, int):
            return ORD[i]
        return jnp.where(i == 3, 2, jnp.where(i == 2, 3, i))

    def piece(i, quarter, j):
        return wt.at[(y + order_at(i)) % 4, quarter, j, core]

    def mine(m, j):
        return m + (0 if j is odd else 2 if j is even else 2 * ((par + j + 1) % 2))

    def other(m, j):
        return m + (2 if j is odd else 0 if j is even else 2 * ((par + j) % 2))

    beside = (z + 1 - 2 * par, (z + 7 + 2 * par) % 8)
    toward, source = (xup, xdn), (xdn, xup)

    def x_copy(way, i, j):
        p = piece(i, x, j)
        return rcopy(p, p, sx.at[way, j, i], rx.at[way, j, i], dev(z, toward[way], y))

    def pair_copy(which, i, j):
        p = piece(i, (x, xdn, xup, xop)[which], j)
        return rcopy(p, p, s2d.at[which, j, i], r2d.at[which, j, i], dev(z, x, y, 1 - core))

    def need(which, i):
        for j in range(2):
            pair_copy(which, i, j).wait_recv()

    def relay_copy(way, j, own=True):
        i = mine(way, j) if own else other(way, j)
        p = piece(i, source[way], j)
        return rcopy(p, p, srl.at[j, i], rrl.at[j, i], dev(z, toward[way], y))

    def zn_copy(w, m, j):
        p = piece(mine(m, j), (xdn, xup, x)[w], j)
        return rcopy(p, p, szp.at[j, w, m], rzp.at[j, w, m], dev(beside[(w + m) % 2], x, y))

    def ready(i, j):
        yy = (y + order_at(i)) % 4
        for n in range(2):
            rcopy(
                zb.at[0, half(n)], wt.at[yy, x, j, core, half(n)], sy.at[0, n],
                ry.at[yy, j, n], dev(z, x, (y + 1) % 4),
            ).wait_recv()

    def x_early(s):
        @pl.when(dist(odd) == s)
        def _():
            ready(0, odd)
            for way in range(2):
                x_copy(way, 0, odd).start()
            zn_copy(2, 0, odd).start()
            pair_copy(0, 0, odd).start()

    def x_stage(s):
        j = odd if s % 2 == 1 else even

        @pl.when(dist(j) == s)
        def _():
            for m in range(s % 2, 2):
                ready(mine(m, j), j)
                for way in range(2):
                    x_copy(way, mine(m, j), j).start()
                zn_copy(2, m, j).start()
                pair_copy(0, mine(m, j), j).start()

    def x_event(j, m):
        for way in (m, 1 - m):
            x_copy(way, mine(m, j), j).wait_recv()
            if way == m:
                relay_copy(way, j).start()
            zn_copy(way, m, j).start()
            pair_copy(1 + way, mine(m, j), j).start()

    def opposite_event(j, way, own=True):
        relay_copy(way, j, own).wait_recv()
        pair_copy(3, mine(way, j) if own else other(way, j), j).start()

    def zn_event(w, m, j):
        zn_copy(w, m, j).wait_recv()
        if w == m:
            relay_copy(w, j, False).start()
        pair_copy((1, 2, 0)[w], other(m, j), j).start()

    yup, ydn, yop = (y + 1) % 4, (y + 3) % 4, (y + 2) % 4

    def chunk(who, n):
        return hidg.at[who, :, pl.ds(n * 256, 256)]

    def h_up(n):
        return rcopy(chunk(y, n), chunk(y, n), shu.at[n], rhu.at[n], dev(z, x, yup))

    def h_dn(n):
        return rcopy(chunk(y, n), chunk(y, n), shd.at[n], rhd.at[n], dev(z, x, ydn))

    def h_relay(n):
        who, to = (ydn, yup) if n < 2 else (yup, ydn)
        return rcopy(chunk(who, n), chunk(who, n), shr.at[n], rhr.at[n], dev(z, x, to))

    def h_relay_in(n):
        return rcopy(
            chunk(yop, n), chunk(yop, n), shr.at[n], rhr.at[n], dev(z, x, yup if n < 2 else ydn)
        )

    def h_event(n):
        h_up(n).wait_recv()
        if n < 2:
            h_relay(n).start()
        h_dn(n).wait_recv()
        if n >= 2:
            h_relay(n).start()

    def unit(who, quarter, start=False):
        t = dot(hidg[who], wt[who, quarter].reshape(384, 1024), 1, 1)
        acc[quarter] = t if start else acc[quarter] + t

    loads[0].wait()
    loads[1].wait()
    col = lax.broadcasted_iota(jnp.int32, (BLK, HD), 0).astype(F32)
    def contribs(h):
        r = rate[h]
        hs = slice(h * HD, (h + 1) * HD)
        kw = jnp.exp(-r * (BLK - 1.0 - col))
        k0 = (k[0:BLK, hs].astype(F32) * kw).astype(BF16)
        k1 = (k[BLK:ROWS, hs].astype(F32) * kw).astype(BF16)
        a0 = dot(k0, v[0:BLK, hs], 0, 0)
        a1 = dot(k1, v[BLK:ROWS, hs], 0, 0)
        c0[h] = a0.astype(BF16)
        loc[h] = (jnp.exp(jnp.full((1, HD), -r * BLK)) * a0 + a1).astype(BF16)

    for h in range(4):
        contribs(h)
    loads[2].wait()
    pl.semaphore_wait(barrier, 17)
    z_start()
    for h in range(4, NH):
        contribs(h)
    rx1[me] = loc[me]
    sends = []
    for d in range(1, 8):
        to = (me + d) % 8
        cp = rcopy(loc.at[to], rx1.at[me], s1.at[d - 1], r1.at[me], (z * 8 + to, y))
        cp.start()
        sends.append(cp)

    loads[3].wait()
    loads[4].wait()
    loads[5].wait()
    ii = lax.broadcasted_iota(jnp.int32, (BLK, BLK), 0)
    jj = lax.broadcasted_iota(jnp.int32, (BLK, BLK), 1)
    off = (ii - jj).astype(F32)

    def intra(h):
        r = rate[h]
        hs = slice(h * HD, (h + 1) * HD)
        decay = jnp.where(off >= 0.0, jnp.exp(-r * jnp.maximum(off, 0.0)), 0.0)
        for b in range(2):
            rs = slice(b * BLK, (b + 1) * BLK)
            w = (dot(q[rs, hs], k[rs, hs], 1, 1) * decay).astype(BF16)
            o = dot(w, v[rs, hs])
            if b == 1:
                o = o + jnp.exp(-r * (col + 1.0)) * dot(q[rs, hs], c0[h])
            u[rs, hs] = o
        gs[:, hs] = jax.nn.sigmoid(g[:, hs].astype(F32)) * gain[:, hs]

    intra(0)
    intra(1)
    z_event(1, 0)
    z_event(1, 1)
    for d in range(1, 8):
        p = (me + 8 - d) % 8
        rcopy(loc.at[0], rx1.at[p], s1.at[0], r1.at[p], (z * 8 + p, y)).wait_recv()
    rm = rate[me]
    d512 = jnp.exp(jnp.full((1, HD), -rm * 512.0))
    e = jnp.zeros((HD, HD), F32)
    for p in range(8):
        exc[p] = e
        e = d512 * e + rx1[p].astype(F32)
    tx2[...] = e.astype(BF16)

    def z_state(d):
        return rcopy(tx2, rx2.at[z], s2.at[d - 1], r2.at[z], ((z + d) % 8 * 8 + me, y))

    for d in range(1, 8):
        @pl.when(z + d < 8)
        def _():
            z_state(d).start()

    intra(2)
    intra(3)
    z_event(2, 0)
    intra(4)
    intra(5)
    z_event(2, 1)
    intra(6)
    intra(7)

    for i in range(7):
        @pl.when(i < z)
        def _():
            rcopy(tx2, rx2.at[i], s2.at[0], r2.at[i], (i * 8 + me, y)).wait_recv()
            tx3[...] = jnp.exp(jnp.full((1, HD), -rm * 4096.0)) * tx3[...] + rx2[i].astype(F32)
    base = tx3[...]
    for p in range(8):
        rx1[p] = (jnp.exp(jnp.full((1, HD), -rm * (512.0 * p))) * base + exc[p]).astype(BF16)
    rx3[me] = rx1[me]
    for d in range(1, 8):
        to = (me + d) % 8
        cp = rcopy(rx1.at[to], rx3.at[me], s3.at[d - 1], r3.at[me], (z * 8 + to, y))
        cp.start()
        sends.append(cp)

    x_early(1)
    z_event(3, 0)
    z_event(3, 1)
    x_early(3)

    row = lax.broadcasted_iota(jnp.int32, (ROWS, HD), 0).astype(F32)
    for h in range(NH):
        @pl.when(h != me)
        def _():
            rcopy(rx1.at[0], rx3.at[h], s3.at[0], r3.at[h], (z * 8 + h, y)).wait_recv()
        hs = slice(h * HD, (h + 1) * HD)
        at = u[:, hs] + jnp.exp(-rate[h] * (row + 1.0)) * dot(q[:, hs], rx3[h])
        scale = lax.rsqrt(jnp.mean(at * at, axis=-1, keepdims=True) + 1e-06)
        hidg[y, :, hs] = (at * scale * gs[:, hs]).astype(BF16)
        if h == 7:
            z_event(4, 0)
            z_event(4, 1)
            for n in range(4):
                h_up(n).start()
                h_dn(n).start()

    x_stage(0)
    x_stage(1)
    x_event(odd, 0)
    x_stage(2)
    x_stage(3)
    x_stage(4)
    def units(i, which):
        for n in which:
            need(n, i)
            unit((y, yup, ydn, yop)[i], (x, xdn, xup, xop)[n], i == 0)

    x_event(odd, 1)
    zn_event(2, 0, even)
    zn_event(0, 0, even)
    zn_event(1, 0, even)
    zn_event(2, 1, even)
    x_event(even, 0)
    zn_event(1, 1, even)
    zn_event(0, 1, even)
    x_event(even, 1)
    units(0, (0, 1, 2))
    h_event(0)
    h_event(1)
    zn_event(2, 0, odd)
    zn_event(0, 0, odd)
    zn_event(1, 0, odd)
    h_event(2)
    zn_event(2, 1, odd)
    zn_event(1, 1, odd)
    zn_event(0, 1, odd)
    h_event(3)
    opposite_event(odd, 0)
    opposite_event(odd, 1)
    opposite_event(even, 0, False)
    opposite_event(even, 1, False)
    units(1, (0, 1, 2))
    opposite_event(even, 0)
    opposite_event(even, 1)
    units(0, (3,))
    units(1, (3,))
    opposite_event(odd, 0, False)
    units(2, (0, 1, 2))
    opposite_event(odd, 1, False)
    units(2, (3,))
    for n in range(3):
        need(n, 3)
    def part(quarter, n):
        ks = slice(n * 256, (n + 1) * 256)
        return dot(hidg[yop, :, ks], wt[yop, quarter, :, :, :, ks].reshape(384, 256), 1, 1)

    h_relay_in(0).wait_recv()
    h_relay_in(2).wait_recv()
    for n, quarter in enumerate((x, xdn, xup, xop)):
        if n == 3:
            need(3, 3)
        acc[quarter] += part(quarter, 0) + part(quarter, 2)
    h_relay_in(1).wait_recv()
    h_relay_in(3).wait_recv()
    for n, quarter in enumerate((x, xdn, xup, xop)):
        res[quarter] = (acc[quarter] + part(quarter, 1) + part(quarter, 3)).astype(BF16)
        pltpu.make_async_copy(res.at[quarter], out.at[quarter], osem.at[n]).start()
    for n, quarter in enumerate((x, xdn, xup, xop)):
        pltpu.make_async_copy(res.at[quarter], out.at[quarter], osem.at[n]).wait()
    for cp in sends:
        cp.wait_send()
    for d in range(1, 8):
        @pl.when(z + d < 8)
        def _():
            z_state(d).wait_send()
    for way in range(2):
        for n in range(2):
            for step in range(4 if way == n else 3):
                z_copy(way, z, n, step).wait_send()
    for zs in range(8):
        rel = (y + 4 - zs // 2) % 4
        far = (z + zs) % 2

        @pl.when(((far == 1) & (rel == 1)) | ((far == 0) & (rel >= 2)))
        def _():
            for n in range(2):
                y_copy(zs, n).wait_send()
    for j in range(2):
        for way in range(2):
            for m in range(2):
                x_copy(way, mine(m, j), j).wait_send()
            relay_copy(way, j).wait_send()
            relay_copy(way, j, False).wait_send()
            for w in range(3):
                zn_copy(w, way, j).wait_send()
        for i in range(4):
            for which in range(4):
                pair_copy(which, i, j).wait_send()
    for n in range(4):
        h_up(n).wait_send()
        h_dn(n).wait_send()
        h_relay(n).wait_send()


def assemble(quarters, out):
    low = lax.broadcasted_iota(jnp.int32, (64, HD), 1) < 64

    def swap(t):
        return pltpu.roll(t, 64, axis=1)

    for pr in range(2):
        for rb in range(8):
            rs = slice(rb * 64, (rb + 1) * 64)
            p0, p1, p2 = (
                quarters[2 * pr, rs, n * HD : (n + 1) * HD].astype(F32) for n in range(3)
            )
            q0, q1, q2 = (
                quarters[2 * pr + 1, rs, n * HD : (n + 1) * HD].astype(F32) for n in range(3)
            )
            sp1, sp2, sq0, sq1 = swap(p1), swap(p2), swap(q0), swap(q1)
            tiles = (
                (p0, jnp.where(low, p1, sq0), jnp.where(low, sq0, sq1)),
                (jnp.where(low, sp1, sp2), jnp.where(low, sp2, q1), q2),
            )
            for j in range(2):
                for n in range(3):
                    at = j * 768 + pr * 384 + n * HD
                    out[rs, at : at + HD] = tiles[j][n].astype(BF16)


def body(
    query_rows, key_rows, value_rows, gate_rows, init_state, decay_rate, norm_gain, out_weight
):
    vm = pl.BlockSpec(memory_space=pltpu.VMEM)
    anyspace = pl.BlockSpec(memory_space=pl.ANY)
    dma = pltpu.SemaphoreType.DMA
    quarters = pl.pallas_call(
        kernel,
        out_shape=jax.ShapeDtypeStruct((4, ROWS, 384), BF16),
        in_specs=[pl.BlockSpec(memory_space=pltpu.SMEM), vm] + [anyspace] * 6,
        out_specs=anyspace,
        scratch_shapes=[
            pltpu.VMEM((ROWS, NH * HD), BF16),
            pltpu.VMEM((ROWS, NH * HD), BF16),
            pltpu.VMEM((ROWS, NH * HD), BF16),
            pltpu.VMEM((ROWS, NH * HD), BF16),
            pltpu.VMEM((ROWS, NH * HD), F32),
            pltpu.VMEM((ROWS, NH * HD), F32),
            pltpu.VMEM((NH, HD, HD), BF16),
            pltpu.VMEM((NH, HD, HD), BF16),
            pltpu.VMEM((8, HD, HD), BF16),
            pltpu.VMEM((8, HD, HD), F32),
            pltpu.VMEM((HD, HD), BF16),
            pltpu.VMEM((8, HD, HD), BF16),
            pltpu.VMEM((HD, HD), F32),
            pltpu.VMEM((NH, HD, HD), BF16),
            pltpu.VMEM((8, 96, 1024), BF16),
            pltpu.VMEM((4, 4, 2, 2, 96, 1024), BF16),
            pltpu.VMEM((4, ROWS, NH * HD), BF16),
            pltpu.VMEM((4, ROWS, 384), F32),
            pltpu.VMEM((4, ROWS, 384), BF16),
            dma((6,)), dma((7,)), dma((8,)), dma((7,)), dma((8,)), dma((7,)), dma((8,)),
            dma((2, 4, 2)), dma((2, 4, 2)), dma((8, 2)), dma((4, 2, 2)),
            dma((2, 2, 4)), dma((2, 2, 4)), dma((2, 4)), dma((2, 4)), dma((2, 3, 2)), dma((2, 3, 2)),
            dma((4, 2, 4)), dma((4, 2, 4)),
            dma((4,)), dma((4,)), dma((4,)), dma((4,)), dma((4,)), dma((4,)), dma((4,)),
        ],
        compiler_params=pltpu.CompilerParams(
            collective_id=0, has_side_effects=True, vmem_limit_bytes=60 * 2**20
        ),
        cost_estimate=pl.CostEstimate(
            flops=8 * 10**9, bytes_accessed=6 * 2**20, transcendentals=10**6
        ),
    )(
        decay_rate, norm_gain[None, :], init_state, query_rows, key_rows, value_rows, gate_rows,
        out_weight.T,
    )
    return pl.pallas_call(
        assemble,
        out_shape=jax.ShapeDtypeStruct((ROWS, 1536), BF16),
        in_specs=[vm],
        out_specs=vm,
    )(quarters)


def solution(mesh):
    return jax.shard_map(
        body,
        mesh=mesh,
        in_specs=(
            P("ctx", "head"),
            P("ctx", "head"),
            P("ctx", "head"),
            P("ctx", "head"),
            P("head", None, None),
            P("head"),
            P("head"),
            P("head", "ctx"),
        ),
        out_specs=P("ctx", "head"),
        check_vma=False,
    )
```
